256 devices in a mesh: dp: 16 (over y, x), tp: 16 (over z, core).
Axes of the slice: x: 4, y: 4, z: 8, core: 2. Of those that a mesh axis runs over, the one named last changes fastest.
Arguments:
- grads: bfloat16 [16, 2, 2560, 5120], P('dp', None, 'tp'), may hold values from -6 to 6
- errors: bfloat16 [16, 2, 2560, 5120], P('dp', None, 'tp'), may hold values from -4 to 4
- basis_in: float32 [2, 2560, 32], P(None, 'tp'), may hold values from -6 to 6
Outputs:
- update: bfloat16 [2, 2560, 5120], P(None, 'tp')
- new_errors: bfloat16 [16, 2, 2560, 5120], P('dp', None, 'tp')
- updated_right_basis: float32 [2, 2560, 32], P(None, 'tp')
The draws below stay inside these ranges and needn't reach their ends.
All inputs are finite; a program needn't handle non-finite values.
Results may differ from the reference program's by a relative error of at most 0.012.
Values sent between devices are 32-bit elements; how exact they have to be, the bound alone decides.
No kernel may reach another device: no remote copies, remote signals or barrier semaphores. Data moves between devices by JAX's collectives and lax.ppermute only.
A program may use at most 64 MiB of HBM per device.

```python
import jax
import jax.numpy as jnp
from jax import lax

D = 5120
HW = 2560
RANK = 32
MATS = 2
HOSTS = 16


def shard_levels(stream_key, dims, shards, smallest, largest):
    def one(axis_at, parts):
        steps = jax.random.uniform(jax.random.fold_in(jax.random.fold_in(stream_key, 6), axis_at), (parts,), jnp.float32, smallest / len(shards), largest / len(shards))
        return jnp.repeat(jnp.exp(steps), dims[axis_at] // parts).reshape((-1,) + (1,) * (len(dims) - axis_at - 1))

    level = one(*shards[0])
    for cut in shards[1:]:
        level = level * one(*cut)
    return level


def noise(own_key, dims, deviation, bound, split=(), kind=jnp.bfloat16):
    values = jax.random.normal(own_key, dims, jnp.float32) * deviation
    if len(split) > 0:
        values = shard_levels(own_key, dims, split, -0.22, 0.18) * values
    return jnp.clip(values, min=-bound, max=bound).astype(kind)


def setup_inputs(seed: int = 0) -> dict:
    streams_of = jax.random.split(jax.random.key(seed), 4)
    grads = noise(streams_of[0], (HOSTS, MATS, HW, D), 1.0, 6.0, ((0, 16), (2, 16)))
    errors = noise(streams_of[1], (HOSTS, MATS, HW, D), 0.5, 4.0, ((0, 16), (2, 16)))
    basis_in = noise(streams_of[2], (MATS, HW, RANK), 1.0, 6.0, ((1, 16),), jnp.float32)
    return dict(grads=grads, errors=errors, basis_in=basis_in)


def orthonormal(summed):
    gram = jnp.einsum('dmr,dms->mrs', summed, summed, precision=lax.Precision.HIGHEST)
    lower = jnp.linalg.cholesky(gram)
    solved = jax.scipy.linalg.solve_triangular(lower, jnp.transpose(summed, (1, 2, 0)), lower=True)
    return jnp.transpose(solved, (2, 0, 1))

def reference(grads, errors, basis_in):
    error_corrected_gradient = (grads.astype(jnp.float32) + errors.astype(jnp.float32)).astype(jnp.bfloat16)
    query_lower_factor = basis_in.astype(jnp.bfloat16)

    def left_term(carry, machine_index):
        product_term = jnp.einsum('tqj,tqw->jtw', machine_index.astype(jnp.float32), query_lower_factor.astype(jnp.float32))
        return (carry + product_term, None)
    start = jnp.zeros((D, MATS, RANK), jnp.float32)
    summed = lax.scan(left_term, start, error_corrected_gradient)[0]
    orthonormal_left = orthonormal(summed)
    orthonormal_lower_factor = orthonormal_left.astype(jnp.bfloat16)

    def right_term(carry, machine_index):
        product_term = jnp.einsum('sct,tsj->scj', machine_index.astype(jnp.float32), orthonormal_lower_factor.astype(jnp.float32))
        return (carry + product_term, None)
    begin = jnp.zeros((MATS, HW, RANK), jnp.float32)
    updated_right_basis = lax.scan(right_term, begin, error_corrected_gradient)[0] / HOSTS
    reconstructed_gradient = jnp.einsum('viz,ibz->ibv', orthonormal_left, updated_right_basis, precision=lax.Precision.HIGHEST)
    update = reconstructed_gradient.astype(jnp.bfloat16)
    new_errors = lax.map(lambda machine_index: (machine_index.astype(jnp.float32) - reconstructed_gradient).astype(jnp.bfloat16), error_corrected_gradient)
    return (update, new_errors, updated_right_basis)
```

```python
import functools

import jax
import jax.numpy as jnp
from jax import lax
from jax.experimental import pallas as pl
from jax.experimental.pallas import tpu as pltpu
from jax.sharding import PartitionSpec as P

D = 5120
ROWS = 160
RANK = 32
HOSTS = 16
CHUNKS = 32
CHUNK_COLS = 640
COL_BLOCKS = D // CHUNK_COLS
AXES = ("dp", "tp")
MIB = 1 << 20


def device(x, y, z, c):
    return (y * 4 + x) * 16 + z * 2 + c


def everyone():
    return [(x, y, z, c) for y in range(4) for x in range(4) for z in range(8) for c in range(2)]


def pairs(move):
    return [(device(*at), device(*move(*at))) for at in everyone()]


CORE_SWAP = pairs(lambda x, y, z, c: (x, y, z, 1 - c))


def z_pairs(k):
    return pairs(lambda x, y, z, c: (x, y, z ^ (2 * k), c))


def first_pairs(k):
    return pairs(lambda x, y, z, c: (x ^ k, y, z, c) if c == 0 else (x, y ^ k, z, c))


def second_pairs(k):
    return pairs(lambda x, y, z, c: (x, y ^ k, z, c) if c == 0 else (x ^ k, y, z, c))


GROUPS = [
    [device(x, y, zz * 2 + k, c) for k in range(2) for y in range(4) for x in range(4)]
    for zz in range(4)
    for c in range(2)
]


def exchange(parts):
    return lax.all_to_all(parts, AXES, 0, 0, axis_index_groups=GROUPS, tiled=True)


def permute(a, perm):
    return lax.ppermute(a, AXES, perm)


def split3(a):
    hi = a.astype(jnp.bfloat16)
    rest = a - hi.astype(jnp.float32)
    mid = rest.astype(jnp.bfloat16)
    lo = (rest - mid.astype(jnp.float32)).astype(jnp.bfloat16)
    return hi, mid, lo


def cost(flops, nbytes):
    return pl.CostEstimate(flops=flops, bytes_accessed=nbytes, transcendentals=0)


def left_kernel(m_ref, grads_ref, errors_ref, basis_ref, corrected_ref, left_ref):
    corrected = (
        grads_ref[0, 0].astype(jnp.float32) + errors_ref[0, 0].astype(jnp.float32)
    ).astype(jnp.bfloat16)
    corrected_ref[...] = corrected
    left = lax.dot_general(
        basis_ref[0].astype(jnp.bfloat16),
        corrected,
        (((0,), (0,)), ((), ())),
        preferred_element_type=jnp.float32,
    )
    blocks = left.shape[1] // CHUNK_COLS
    for b in range(blocks):
        for g in range(4):
            left_ref[b * 4 + g] = left[8 * g : 8 * g + 8, b * CHUNK_COLS : (b + 1) * CHUNK_COLS]


def left_part(m, grads, errors, basis, steps=4):
    cols = D // steps
    return pl.pallas_call(
        left_kernel,
        grid_spec=pltpu.PrefetchScalarGridSpec(
            num_scalar_prefetch=1,
            grid=(steps,),
            in_specs=[
                pl.BlockSpec((1, 1, ROWS, cols), lambda j, m: (0, m[0], 0, j)),
                pl.BlockSpec((1, 1, ROWS, cols), lambda j, m: (0, m[0], 0, j)),
                pl.BlockSpec((1, ROWS, RANK), lambda j, m: (m[0], 0, 0)),
            ],
            out_specs=[
                pl.BlockSpec((ROWS, cols), lambda j, m: (0, j)),
                pl.BlockSpec((CHUNKS // steps, 8, CHUNK_COLS), lambda j, m: (j, 0, 0)),
            ],
        ),
        out_shape=[
            jax.ShapeDtypeStruct((ROWS, D), jnp.bfloat16),
            jax.ShapeDtypeStruct((CHUNKS, 8, CHUNK_COLS), jnp.float32),
        ],
        compiler_params=pltpu.CompilerParams(vmem_limit_bytes=16 * MIB),
        cost_estimate=cost(2 * ROWS * D * RANK, 6 * ROWS * D + 4 * RANK * D),
        name="left",
    )(m, grads, errors, basis)


def right_body(left_ref, corrected_ref, terms_ref, stack_ref):
    for b in range(COL_BLOCKS):
        cols = slice(b * CHUNK_COLS, (b + 1) * CHUNK_COLS)
        for g in range(4):
            rows = slice(8 * g, 8 * g + 8)
            stack_ref[rows, cols] = left_ref[b * 4 + g]
    for b in range(COL_BLOCKS):
        cols = slice(b * CHUNK_COLS, (b + 1) * CHUNK_COLS)
        hi, mid, lo = split3(stack_ref[:, cols])
        for i, term in enumerate((hi, mid, lo, hi, mid, hi)):
            terms_ref[i * RANK : (i + 1) * RANK, cols] = term
    terms = terms_ref[0 : 3 * RANK, :]
    nt = (((1,), (1,)), ((), ()))
    t = lax.dot_general(corrected_ref[...], terms, nt, preferred_element_type=jnp.float32)
    t = t[:, 0:RANK] + (t[:, RANK : 2 * RANK] + t[:, 2 * RANK : 3 * RANK])
    packed = jnp.concatenate([t[40 * i : 40 * i + 40] for i in range(4)], axis=1)
    g = lax.dot_general(terms, terms, nt, preferred_element_type=jnp.float32)
    gram = g[0:RANK, 0:RANK]
    rest = jnp.zeros_like(gram)
    for i in range(3):
        for j in range(3):
            if i + j > 0:
                rest = rest + g[i * RANK : (i + 1) * RANK, j * RANK : (j + 1) * RANK]
    return packed, gram + rest


def right_kernel(left_ref, corrected_ref, t_ref, gram_ref, terms_ref, stack_ref):
    t_ref[...], gram_ref[...] = right_body(left_ref, corrected_ref, terms_ref, stack_ref)


def right_both_kernel(
    left_ref, corrected_ref, t_own_ref, gram_own_ref, t_ref, gram_ref, terms_ref, stack_ref
):
    t, gram = right_body(left_ref, corrected_ref, terms_ref, stack_ref)
    t_ref[0:40] = t_own_ref[...]
    t_ref[40:80] = t
    gram_ref[0] = gram_own_ref[...]
    gram_ref[1] = gram


def vmem(n):
    return [pl.BlockSpec(memory_space=pltpu.VMEM)] * n


def right_part(left, corrected, own=None):
    both = own is not None
    n = 2 if both else 1
    return pl.pallas_call(
        right_both_kernel if both else right_kernel,
        in_specs=vmem(4 if both else 2),
        out_specs=vmem(3),
        out_shape=[
            jax.ShapeDtypeStruct((40 * n, 128), jnp.float32),
            jax.ShapeDtypeStruct((2, RANK, RANK) if both else (RANK, RANK), jnp.float32),
            jax.ShapeDtypeStruct((6 * RANK, D), jnp.bfloat16),
        ],
        scratch_shapes=[pltpu.VMEM((RANK, D), jnp.float32)],
        compiler_params=pltpu.CompilerParams(vmem_limit_bytes=24 * MIB),
        cost_estimate=cost(2 * 256 * D * 96, 2 * ROWS * D + 16 * RANK * D),
        name="right",
    )(left, corrected, *(own or ()))


def inverse_kernel(gram_ref, inverse_ref):
    row = lax.broadcasted_iota(jnp.int32, (RANK, RANK), 0)
    col = lax.broadcasted_iota(jnp.int32, (RANK, RANK), 1)
    eye = jnp.where(row == col, 1.0, 0.0).astype(jnp.float32)
    a = jnp.concatenate([gram_ref[0], eye, gram_ref[1], eye], axis=1)
    rows = lax.broadcasted_iota(jnp.int32, (RANK, 4 * RANK), 0)
    lanes = lax.broadcasted_iota(jnp.int32, (RANK, 4 * RANK), 1)
    first = lanes < 2 * RANK
    for k in range(RANK):
        left = jnp.broadcast_to(a[:, k : k + 1], a.shape)
        right = jnp.broadcast_to(a[:, 2 * RANK + k : 2 * RANK + k + 1], a.shape)
        column = jnp.where(first, left, right)
        scale = lax.rsqrt(column[k : k + 1, :])
        pivot_row = a[k : k + 1, :] * scale
        below = jnp.where(rows > k, column * scale, 0.0)
        a = jnp.where(rows == k, pivot_row, a - below * pivot_row)
    inverse_ref[0] = a[:, RANK : 2 * RANK]
    inverse_ref[1] = a[:, 3 * RANK : 4 * RANK]


def inverses(gram):
    return pl.pallas_call(
        inverse_kernel,
        in_specs=vmem(1),
        out_specs=pl.BlockSpec(memory_space=pltpu.VMEM),
        out_shape=jax.ShapeDtypeStruct((2, RANK, RANK), jnp.float32),
        compiler_params=pltpu.CompilerParams(vmem_limit_bytes=4 * MIB),
        cost_estimate=cost(10_000_000, 8_000_000),
        name="inverse",
    )(gram)


def final_kernel(
    c_ref,
    t0_ref,
    t1_ref,
    t2_ref,
    t3_ref,
    inverse_ref,
    terms_own_ref,
    terms_other_ref,
    corrected_own_ref,
    corrected_other_ref,
    update_ref,
    errors_ref,
    right_ref,
    w_ref,
):
    high = functools.partial(
        lax.dot_general, precision=lax.Precision.HIGHEST, preferred_element_type=jnp.float32
    )
    i = pl.program_id(0)
    j = pl.program_id(1)

    @pl.when((i == 0) & (j == 0))
    def _():
        t = (t0_ref[...] + t1_ref[...]) + (t2_ref[...] + t3_ref[...])
        for n in range(2):
            mine = t[40 * n : 40 * n + 40]
            mine = jnp.concatenate(
                [mine[:, RANK * q : RANK * q + RANK] for q in range(4)], axis=0
            )
            inverse = inverse_ref[n]
            right = high(mine, inverse, (((1,), (1,)), ((), ()))) * (1.0 / HOSTS)
            right_ref[c_ref[n]] = right
            hi, mid, lo = split3(high(right, inverse, (((1,), (0,)), ((), ()))))
            w_ref[n] = jnp.concatenate([hi, hi, hi, mid, mid, lo], axis=1)

    def finish(terms_ref, corrected_ref, n):
        recon = jnp.dot(w_ref[n], terms_ref[...], preferred_element_type=jnp.float32)
        update_ref[0] = recon.astype(jnp.bfloat16)
        errors_ref[0, 0] = (corrected_ref[...].astype(jnp.float32) - recon).astype(jnp.bfloat16)

    @pl.when(i == 0)
    def _():
        finish(terms_own_ref, corrected_own_ref, 0)

    @pl.when(i == 1)
    def _():
        finish(terms_other_ref, corrected_other_ref, 1)


def final_part(order, ts, inverse, terms_own, terms_other, corrected_own, corrected_other, steps=4):
    cols = D // steps
    own = lambda i, j, c: (0, jnp.where(i == 0, j, steps - 1))
    other = lambda i, j, c: (0, jnp.where(i == 0, 0, j))
    whole = [pl.BlockSpec((80, 128), lambda i, j, c: (0, 0))] * 4
    return pl.pallas_call(
        final_kernel,
        grid_spec=pltpu.PrefetchScalarGridSpec(
            num_scalar_prefetch=1,
            grid=(2, steps),
            in_specs=whole
            + [
                pl.BlockSpec((2, RANK, RANK), lambda i, j, c: (0, 0, 0)),
                pl.BlockSpec((6 * RANK, cols), own),
                pl.BlockSpec((6 * RANK, cols), other),
                pl.BlockSpec((ROWS, cols), own),
                pl.BlockSpec((ROWS, cols), other),
            ],
            out_specs=[
                pl.BlockSpec((1, ROWS, cols), lambda i, j, c: (c[i], 0, j)),
                pl.BlockSpec((1, 1, ROWS, cols), lambda i, j, c: (0, c[i], 0, j)),
                pl.BlockSpec((2, ROWS, RANK), lambda i, j, c: (0, 0, 0)),
            ],
            scratch_shapes=[pltpu.VMEM((2, ROWS, 6 * RANK), jnp.bfloat16)],
        ),
        out_shape=[
            jax.ShapeDtypeStruct((2, ROWS, D), jnp.bfloat16),
            jax.ShapeDtypeStruct((1, 2, ROWS, D), jnp.bfloat16),
            jax.ShapeDtypeStruct((2, ROWS, RANK), jnp.float32),
        ],
        compiler_params=pltpu.CompilerParams(vmem_limit_bytes=24 * MIB),
        cost_estimate=cost(2 * 2 * ROWS * 192 * D, 16 * ROWS * D),
        name="final",
    )(order, *ts, inverse, terms_own, terms_other, corrected_own, corrected_other)


def on_device(grads, errors, basis_in):
    core = lax.rem(lax.axis_index("tp"), 2).astype(jnp.int32)
    corrected_other, left_other = left_part((1 - core)[None], grads, errors, basis_in)
    with jax.named_scope("left_core_swap"):
        arrived = permute(left_other, CORE_SWAP)
    corrected_own, left_own = left_part(core[None], grads, errors, basis_in)
    with jax.named_scope("left_sum"):
        parts = exchange(left_own + arrived)
        part = jnp.sum(parts, axis=0)
        p1, p3, p2 = (permute(part, z_pairs(k)) for k in (1, 3, 2))
        part = (part + p1) + (p2 + p3)
        left_own = exchange(jnp.broadcast_to(part[None], (CHUNKS,) + part.shape))
        left_other = permute(left_own, CORE_SWAP)
    t_own, gram_own, terms_own = right_part(left_own, corrected_own)
    t, gram, terms_other = right_part(left_other, corrected_other, (t_own, gram_own))
    with jax.named_scope("right_sum"):
        t1, t3, t2 = (permute(t, first_pairs(k)) for k in (1, 3, 2))
        t = (t + t1) + (t2 + t3)
        t1, t3, t2 = (permute(t, second_pairs(k)) for k in (1, 3, 2))
    inverse = inverses(gram)
    order = jnp.stack([core, 1 - core])
    return tuple(
        final_part(
            order, (t, t1, t2, t3), inverse, terms_own, terms_other, corrected_own, corrected_other
        )
    )


def solution(mesh):
    return jax.shard_map(
        on_device,
        mesh=mesh,
        in_specs=(P("dp", None, "tp", None), P("dp", None, "tp", None), P(None, "tp", None)),
        out_specs=(P(None, "tp", None), P("dp", None, "tp", None), P(None, "tp", None)),
        check_vma=False,
    )
```

```python
import functools

import jax
import jax.numpy as jnp
from jax import lax
from jax.experimental import pallas as pl
from jax.experimental.pallas import tpu as pltpu
from jax.sharding import PartitionSpec as P

D = 5120
ROWS = 160
RANK = 32
HOSTS = 16
CHUNKS = 32
CHUNK_COLS = 640
COL_BLOCKS = D // CHUNK_COLS
AXES = ("dp", "tp")
MIB = 1 << 20


def device(x, y, z, c):
    return (y * 4 + x) * 16 + z * 2 + c


def everyone():
    return [(x, y, z, c) for y in range(4) for x in range(4) for z in range(8) for c in range(2)]


def pairs(move):
    return [(device(*at), device(*move(*at))) for at in everyone()]


CORE_SWAP = pairs(lambda x, y, z, c: (x, y, z, 1 - c))


def z_pairs(k):
    return pairs(lambda x, y, z, c: (x, y, z ^ (2 * k), c))


def first_pairs(k):
    return pairs(lambda x, y, z, c: (x ^ k, y, z, c) if c == 0 else (x, y ^ k, z, c))


def second_pairs(k):
    return pairs(lambda x, y, z, c: (x, y ^ k, z, c) if c == 0 else (x ^ k, y, z, c))


GROUPS = [
    [device(x, y, zz * 2 + k, c) for k in range(2) for y in range(4) for x in range(4)]
    for zz in range(4)
    for c in range(2)
]


def exchange(parts):
    return lax.all_to_all(parts, AXES, 0, 0, axis_index_groups=GROUPS, tiled=True)


def permute(a, perm):
    return lax.ppermute(a, AXES, perm)


def split3(a):
    hi = a.astype(jnp.bfloat16)
    rest = a - hi.astype(jnp.float32)
    mid = rest.astype(jnp.bfloat16)
    lo = (rest - mid.astype(jnp.float32)).astype(jnp.bfloat16)
    return hi, mid, lo


def cost(flops, nbytes):
    return pl.CostEstimate(flops=flops, bytes_accessed=nbytes, transcendentals=0)


def vmem(n):
    return [pl.BlockSpec(memory_space=pltpu.VMEM)] * n


def left_kernel(m_ref, grads_ref, errors_ref, basis_ref, corrected_ref, left_ref, *scratch):
    grads_at, errors_at, basis_at, sems, basis_sem = scratch
    m = m_ref[0]
    basis_copy = pltpu.make_async_copy(basis_ref.at[m], basis_at, basis_sem)
    basis_copy.start()
    copies = []
    for b in range(COL_BLOCKS):
        cols = pl.ds(b * CHUNK_COLS, CHUNK_COLS)
        pair = (
            pltpu.make_async_copy(grads_ref.at[0, m, :, cols], grads_at.at[b], sems.at[b, 0]),
            pltpu.make_async_copy(errors_ref.at[0, m, :, cols], errors_at.at[b], sems.at[b, 1]),
        )
        for copy in pair:
            copy.start()
        copies.append(pair)
    basis_copy.wait()
    basis = basis_at[...].astype(jnp.bfloat16)
    for b in range(COL_BLOCKS):
        for copy in copies[b]:
            copy.wait()
        corrected = (
            grads_at[b].astype(jnp.float32) + errors_at[b].astype(jnp.float32)
        ).astype(jnp.bfloat16)
        corrected_ref[:, b * CHUNK_COLS : (b + 1) * CHUNK_COLS] = corrected
        left = jnp.dot(basis, corrected, preferred_element_type=jnp.float32)
        for g in range(4):
            left_ref[b * 4 + g] = left[8 * g : 8 * g + 8]


def left_part(m, grads, errors, basis):
    return pl.pallas_call(
        left_kernel,
        in_specs=[
            pl.BlockSpec(memory_space=pltpu.SMEM),
        ]
        + [pl.BlockSpec(memory_space=pltpu.HBM)] * 3,
        out_specs=vmem(2),
        out_shape=[
            jax.ShapeDtypeStruct((ROWS, D), jnp.bfloat16),
            jax.ShapeDtypeStruct((CHUNKS, 8, CHUNK_COLS), jnp.float32),
        ],
        scratch_shapes=[
            pltpu.VMEM((COL_BLOCKS, ROWS, CHUNK_COLS), jnp.bfloat16),
            pltpu.VMEM((COL_BLOCKS, ROWS, CHUNK_COLS), jnp.bfloat16),
            pltpu.VMEM((RANK, ROWS), jnp.float32),
            pltpu.SemaphoreType.DMA((COL_BLOCKS, 2)),
            pltpu.SemaphoreType.DMA(()),
        ],
        compiler_params=pltpu.CompilerParams(vmem_limit_bytes=16 * MIB),
        cost_estimate=cost(2 * ROWS * D * RANK, 6 * ROWS * D + 4 * RANK * D),
        name="left",
    )(m, grads, errors, basis)


def add_up_kernel(parts_ref, sum_ref):
    parts = [parts_ref[k] for k in range(CHUNKS)]
    while len(parts) > 1:
        parts = [parts[k] + parts[k + 1] for k in range(0, len(parts), 2)]
    sum_ref[...] = parts[0]


def add_up(parts):
    return pl.pallas_call(
        add_up_kernel,
        in_specs=vmem(1),
        out_specs=pl.BlockSpec(memory_space=pltpu.VMEM),
        out_shape=jax.ShapeDtypeStruct((8, CHUNK_COLS), jnp.float32),
        compiler_params=pltpu.CompilerParams(vmem_limit_bytes=4 * MIB),
        cost_estimate=cost(CHUNKS * 8 * CHUNK_COLS, 4 * CHUNKS * 8 * CHUNK_COLS),
        name="add_up",
    )(parts)


def right_body(left_ref, corrected_ref, terms_ref, stack_ref):
    for b in range(COL_BLOCKS):
        cols = slice(b * CHUNK_COLS, (b + 1) * CHUNK_COLS)
        for g in range(4):
            rows = slice(8 * g, 8 * g + 8)
            stack_ref[rows, cols] = left_ref[b * 4 + g]
    for b in range(COL_BLOCKS):
        cols = slice(b * CHUNK_COLS, (b + 1) * CHUNK_COLS)
        hi, mid, lo = split3(stack_ref[:, cols])
        for i, term in enumerate((hi, mid, lo, hi, mid, hi)):
            terms_ref[i * RANK : (i + 1) * RANK, cols] = term
    terms = terms_ref[0 : 3 * RANK, :]
    nt = (((1,), (1,)), ((), ()))
    t = lax.dot_general(corrected_ref[...], terms, nt, preferred_element_type=jnp.float32)
    t = t[:, 0:RANK] + (t[:, RANK : 2 * RANK] + t[:, 2 * RANK : 3 * RANK])
    packed = jnp.concatenate([t[40 * i : 40 * i + 40] for i in range(4)], axis=1)
    g = lax.dot_general(terms, terms, nt, preferred_element_type=jnp.float32)
    gram = g[0:RANK, 0:RANK]
    rest = jnp.zeros_like(gram)
    for i in range(3):
        for j in range(3):
            if i + j > 0:
                rest = rest + g[i * RANK : (i + 1) * RANK, j * RANK : (j + 1) * RANK]
    return packed, gram + rest


def right_kernel(left_ref, corrected_ref, t_ref, gram_ref, terms_ref, stack_ref):
    t_ref[...], gram_ref[...] = right_body(left_ref, corrected_ref, terms_ref, stack_ref)


def right_both_kernel(
    left_ref, corrected_ref, t_own_ref, gram_own_ref, t_ref, gram_ref, terms_ref, stack_ref
):
    t, gram = right_body(left_ref, corrected_ref, terms_ref, stack_ref)
    t_ref[0:40] = t_own_ref[...]
    t_ref[40:80] = t
    gram_ref[0] = gram_own_ref[...]
    gram_ref[1] = gram


def right_part(left, corrected, own=None):
    both = own is not None
    n = 2 if both else 1
    return pl.pallas_call(
        right_both_kernel if both else right_kernel,
        in_specs=vmem(4 if both else 2),
        out_specs=vmem(3),
        out_shape=[
            jax.ShapeDtypeStruct((40 * n, 128), jnp.float32),
            jax.ShapeDtypeStruct((2, RANK, RANK) if both else (RANK, RANK), jnp.float32),
            jax.ShapeDtypeStruct((6 * RANK, D), jnp.bfloat16),
        ],
        scratch_shapes=[pltpu.VMEM((RANK, D), jnp.float32)],
        compiler_params=pltpu.CompilerParams(vmem_limit_bytes=24 * MIB),
        cost_estimate=cost(2 * 256 * D * 96, 2 * ROWS * D + 16 * RANK * D),
        name="right",
    )(left, corrected, *(own or ()))


def inverse_kernel(gram_ref, inverse_ref):
    row = lax.broadcasted_iota(jnp.int32, (RANK, RANK), 0)
    col = lax.broadcasted_iota(jnp.int32, (RANK, RANK), 1)
    eye = jnp.where(row == col, 1.0, 0.0).astype(jnp.float32)
    a = jnp.concatenate([gram_ref[0], eye, gram_ref[1], eye], axis=1)
    rows = lax.broadcasted_iota(jnp.int32, a.shape, 0)
    first = lax.broadcasted_iota(jnp.int32, a.shape, 1) < 2 * RANK
    for base in range(0, RANK, 4):
        below, across = [], []
        for k in range(base, base + 4):
            left = jnp.broadcast_to(a[:, k : k + 1], a.shape)
            right = jnp.broadcast_to(a[:, 2 * RANK + k : 2 * RANK + k + 1], a.shape)
            below.append(jnp.where(first, left, right))
            across.append(a[k : k + 1, :])
        done = a
        for p in range(4):
            k = base + p
            scale = lax.rsqrt(below[p][k : k + 1, :])
            below[p] = below[p] * scale
            across[p] = across[p] * scale
            for q in range(p + 1, 4):
                factor = below[p][base + q : base + q + 1, :]
                below[q] = below[q] - below[p] * factor
                across[q] = across[q] - factor * across[p]
            a = a - below[p] * across[p]
            done = jnp.where(rows == k, across[p], done)
        a = jnp.where(rows >= base + 4, a, done)
    inverse_ref[0] = a[:, RANK : 2 * RANK]
    inverse_ref[1] = a[:, 3 * RANK : 4 * RANK]


def inverses(gram):
    return pl.pallas_call(
        inverse_kernel,
        in_specs=vmem(1),
        out_specs=pl.BlockSpec(memory_space=pltpu.VMEM),
        out_shape=jax.ShapeDtypeStruct((2, RANK, RANK), jnp.float32),
        compiler_params=pltpu.CompilerParams(vmem_limit_bytes=4 * MIB),
        cost_estimate=cost(10_000_000, 8_000_000),
        name="inverse",
    )(gram)


def final_kernel(
    core_ref,
    t0_ref,
    t1_ref,
    t2_ref,
    t3_ref,
    inverse_ref,
    terms_own_ref,
    terms_other_ref,
    corrected_own_ref,
    corrected_other_ref,
    update_ref,
    errors_ref,
    right_ref,
    update_at,
    errors_at,
    sems,
):
    high = functools.partial(
        lax.dot_general, precision=lax.Precision.HIGHEST, preferred_element_type=jnp.float32
    )
    nt = (((1,), (1,)), ((), ()))
    nn = (((1,), (0,)), ((), ()))
    core = core_ref[0]
    t = (t0_ref[...] + t1_ref[...]) + (t2_ref[...] + t3_ref[...])
    t = t * (1.0 / HOSTS)
    copies = []
    for n in range(2):
        m = core if n == 0 else 1 - core
        terms_ref = (terms_own_ref, terms_other_ref)[n]
        corrected_ref = (corrected_own_ref, corrected_other_ref)[n]
        mine = t[40 * n : 40 * n + 40]
        mine = jnp.concatenate([mine[:, RANK * q : RANK * q + RANK] for q in range(4)], axis=0)
        inverse = inverse_ref[n]
        right_ref[m] = high(inverse, mine, nt)
        hi, mid, lo = split3(high(high(mine, inverse, nt), inverse, nn))
        w = jnp.concatenate([hi, hi, hi, mid, mid, lo], axis=1)
        for b in range(COL_BLOCKS):
            cols = slice(b * CHUNK_COLS, (b + 1) * CHUNK_COLS)
            recon = jnp.dot(w, terms_ref[:, cols], preferred_element_type=jnp.float32)
            update_at[n, b] = recon.astype(jnp.bfloat16)
            errors_at[n, b] = (corrected_ref[:, cols].astype(jnp.float32) - recon).astype(
                jnp.bfloat16
            )
            there = pl.ds(b * CHUNK_COLS, CHUNK_COLS)
            pair = (
                pltpu.make_async_copy(
                    update_at.at[n, b], update_ref.at[m, :, there], sems.at[n, b, 0]
                ),
                pltpu.make_async_copy(
                    errors_at.at[n, b], errors_ref.at[0, m, :, there], sems.at[n, b, 1]
                ),
            )
            for copy in pair:
                copy.start()
            copies.extend(pair)
    for copy in copies:
        copy.wait()


def final_part(core, ts, inverse, terms_own, terms_other, corrected_own, corrected_other):
    hbm = pl.BlockSpec(memory_space=pltpu.HBM)
    return pl.pallas_call(
        final_kernel,
        in_specs=[pl.BlockSpec(memory_space=pltpu.SMEM)] + vmem(9),
        out_specs=[hbm, hbm, pl.BlockSpec(memory_space=pltpu.VMEM)],
        out_shape=[
            jax.ShapeDtypeStruct((2, ROWS, D), jnp.bfloat16),
            jax.ShapeDtypeStruct((1, 2, ROWS, D), jnp.bfloat16),
            jax.ShapeDtypeStruct((2, RANK, ROWS), jnp.float32),
        ],
        scratch_shapes=[
            pltpu.VMEM((2, COL_BLOCKS, ROWS, CHUNK_COLS), jnp.bfloat16),
            pltpu.VMEM((2, COL_BLOCKS, ROWS, CHUNK_COLS), jnp.bfloat16),
            pltpu.SemaphoreType.DMA((2, COL_BLOCKS, 2)),
        ],
        compiler_params=pltpu.CompilerParams(vmem_limit_bytes=24 * MIB),
        cost_estimate=cost(2 * 2 * ROWS * 192 * D, 16 * ROWS * D),
        name="final",
    )(core, *ts, inverse, terms_own, terms_other, corrected_own, corrected_other)


def on_device(grads, errors, basis_in):
    core = lax.rem(lax.axis_index("tp"), 2).astype(jnp.int32)
    grads, errors, basis = (
        pltpu.with_memory_space_constraint(a, pltpu.HBM)
        for a in (grads, errors, jnp.swapaxes(basis_in, 1, 2))
    )
    corrected_other, left_other = left_part((1 - core)[None], grads, errors, basis)
    with jax.named_scope("left_core_swap"):
        arrived = permute(left_other, CORE_SWAP)
    corrected_own, left_own = left_part(core[None], grads, errors, basis)
    with jax.named_scope("left_sum"):
        parts = exchange(left_own + arrived)
        part = add_up(parts)
        p1, p3, p2 = (permute(part, z_pairs(k)) for k in (1, 3, 2))
        part = (part + p1) + (p2 + p3)
        left_own = exchange(jnp.broadcast_to(part[None], (CHUNKS,) + part.shape))
        left_other = permute(left_own, CORE_SWAP)
    t_own, gram_own, terms_own = right_part(left_own, corrected_own)
    t, gram, terms_other = right_part(left_other, corrected_other, (t_own, gram_own))
    with jax.named_scope("right_sum"):
        t1, t3, t2 = (permute(t, first_pairs(k)) for k in (1, 3, 2))
        t = (t + t1) + (t2 + t3)
        t1, t3, t2 = (permute(t, second_pairs(k)) for k in (1, 3, 2))
    inverse = inverses(gram)
    update, new_errors, right = final_part(
        core[None], (t, t1, t2, t3), inverse, terms_own, terms_other, corrected_own, corrected_other
    )
    return update, new_errors, jnp.swapaxes(right, 1, 2)


def solution(mesh):
    return jax.shard_map(
        on_device,
        mesh=mesh,
        in_specs=(P("dp", None, "tp", None), P("dp", None, "tp", None), P(None, "tp", None)),
        out_specs=(P(None, "tp", None), P("dp", None, "tp", None), P(None, "tp", None)),
        check_vma=False,
    )
```

```python
import functools

import jax
import jax.numpy as jnp
from jax import lax
from jax.experimental import pallas as pl
from jax.experimental.pallas import tpu as pltpu
from jax.sharding import PartitionSpec as P

D = 5120
ROWS = 160
RANK = 32
HOSTS = 16
CHUNKS = 32
CHUNK_COLS = 640
COL_BLOCKS = D // CHUNK_COLS
AXES = ("dp", "tp")
MIB = 1 << 20


def device(x, y, z, c):
    return (y * 4 + x) * 16 + z * 2 + c


def everyone():
    return [(x, y, z, c) for y in range(4) for x in range(4) for z in range(8) for c in range(2)]


def pairs(move):
    return [(device(*at), device(*move(*at))) for at in everyone()]


CORE_SWAP = pairs(lambda x, y, z, c: (x, y, z, 1 - c))


def z_pairs(k):
    return pairs(lambda x, y, z, c: (x, y, z ^ (2 * k), c))


def first_pairs(k):
    return pairs(lambda x, y, z, c: (x ^ k, y, z, c) if c == 0 else (x, y ^ k, z, c))


def second_pairs(k):
    return pairs(lambda x, y, z, c: (x, y ^ k, z, c) if c == 0 else (x ^ k, y, z, c))


GROUPS = [
    [device(x, y, zz * 2 + k, c) for k in range(2) for y in range(4) for x in range(4)]
    for zz in range(4)
    for c in range(2)
]


def exchange(parts):
    return lax.all_to_all(parts, AXES, 0, 0, axis_index_groups=GROUPS, tiled=True)


def permute(a, perm):
    return lax.ppermute(a, AXES, perm)


def split3(a):
    hi = a.astype(jnp.bfloat16)
    rest = a - hi.astype(jnp.float32)
    mid = rest.astype(jnp.bfloat16)
    lo = (rest - mid.astype(jnp.float32)).astype(jnp.bfloat16)
    return hi, mid, lo


def cost(flops, nbytes):
    return pl.CostEstimate(flops=flops, bytes_accessed=nbytes, transcendentals=0)


def vmem(n):
    return [pl.BlockSpec(memory_space=pltpu.VMEM)] * n


def left_kernel(m_ref, grads_ref, errors_ref, basis_ref, corrected_ref, left_ref, *scratch):
    grads_at, errors_at, basis_at, sems, basis_sem = scratch
    m = m_ref[0]
    basis_copy = pltpu.make_async_copy(basis_ref.at[m], basis_at, basis_sem)
    basis_copy.start()
    copies = []
    for b in range(2):
        cols = pl.ds(b * (D // 2), D // 2)
        pair = (
            pltpu.make_async_copy(grads_ref.at[0, m, :, cols], grads_at.at[:, cols], sems.at[b, 0]),
            pltpu.make_async_copy(
                errors_ref.at[0, m, :, cols], errors_at.at[:, cols], sems.at[b, 1]
            ),
        )
        for copy in pair:
            copy.start()
        copies.append(pair)
    basis_copy.wait()
    basis = basis_at[...].astype(jnp.bfloat16)
    for b in range(COL_BLOCKS):
        if b % (COL_BLOCKS // 2) == 0:
            for copy in copies[b // (COL_BLOCKS // 2)]:
                copy.wait()
        cols = slice(b * CHUNK_COLS, (b + 1) * CHUNK_COLS)
        corrected = (
            grads_at[:, cols].astype(jnp.float32) + errors_at[:, cols].astype(jnp.float32)
        ).astype(jnp.bfloat16)
        corrected_ref[:, cols] = corrected
        left = jnp.dot(basis, corrected, preferred_element_type=jnp.float32)
        for g in range(4):
            left_ref[b * 4 + g] = left[8 * g : 8 * g + 8]


def left_part(m, grads, errors, basis):
    return pl.pallas_call(
        left_kernel,
        in_specs=[
            pl.BlockSpec(memory_space=pltpu.SMEM),
        ]
        + [pl.BlockSpec(memory_space=pltpu.HBM)] * 3,
        out_specs=vmem(2),
        out_shape=[
            jax.ShapeDtypeStruct((ROWS, D), jnp.bfloat16),
            jax.ShapeDtypeStruct((CHUNKS, 8, CHUNK_COLS), jnp.float32),
        ],
        scratch_shapes=[
            pltpu.VMEM((ROWS, D), jnp.bfloat16),
            pltpu.VMEM((ROWS, D), jnp.bfloat16),
            pltpu.VMEM((RANK, ROWS), jnp.float32),
            pltpu.SemaphoreType.DMA((2, 2)),
            pltpu.SemaphoreType.DMA(()),
        ],
        compiler_params=pltpu.CompilerParams(vmem_limit_bytes=16 * MIB),
        cost_estimate=cost(2 * ROWS * D * RANK, 6 * ROWS * D + 4 * RANK * D),
        name="left",
    )(m, grads, errors, basis)


def add_up_kernel(parts_ref, sum_ref):
    parts = [parts_ref[k] for k in range(CHUNKS)]
    while len(parts) > 1:
        parts = [parts[k] + parts[k + 1] for k in range(0, len(parts), 2)]
    sum_ref[...] = parts[0]


def add_up(parts):
    return pl.pallas_call(
        add_up_kernel,
        in_specs=vmem(1),
        out_specs=pl.BlockSpec(memory_space=pltpu.VMEM),
        out_shape=jax.ShapeDtypeStruct((8, CHUNK_COLS), jnp.float32),
        compiler_params=pltpu.CompilerParams(vmem_limit_bytes=4 * MIB),
        cost_estimate=cost(CHUNKS * 8 * CHUNK_COLS, 4 * CHUNKS * 8 * CHUNK_COLS),
        name="add_up",
    )(parts)


def right_body(left_ref, corrected_ref, terms_ref, stack_ref):
    for b in range(COL_BLOCKS):
        cols = slice(b * CHUNK_COLS, (b + 1) * CHUNK_COLS)
        for g in range(4):
            rows = slice(8 * g, 8 * g + 8)
            stack_ref[rows, cols] = left_ref[b * 4 + g]
    for b in range(COL_BLOCKS):
        cols = slice(b * CHUNK_COLS, (b + 1) * CHUNK_COLS)
        hi, mid, lo = split3(stack_ref[:, cols])
        for i, term in enumerate((hi, mid, lo, hi, mid, hi)):
            terms_ref[i * RANK : (i + 1) * RANK, cols] = term
    terms = terms_ref[0 : 3 * RANK, :]
    nt = (((1,), (1,)), ((), ()))
    t = lax.dot_general(corrected_ref[...], terms, nt, preferred_element_type=jnp.float32)
    t = t[:, 0:RANK] + (t[:, RANK : 2 * RANK] + t[:, 2 * RANK : 3 * RANK])
    packed = jnp.concatenate([t[40 * i : 40 * i + 40] for i in range(4)], axis=1)
    g = lax.dot_general(terms, terms, nt, preferred_element_type=jnp.float32)
    gram = g[0:RANK, 0:RANK]
    rest = jnp.zeros_like(gram)
    for i in range(3):
        for j in range(3):
            if i + j > 0:
                rest = rest + g[i * RANK : (i + 1) * RANK, j * RANK : (j + 1) * RANK]
    return packed, gram + rest


def right_kernel(left_ref, corrected_ref, t_ref, gram_ref, terms_ref, stack_ref):
    t_ref[...], gram_ref[...] = right_body(left_ref, corrected_ref, terms_ref, stack_ref)


def right_both_kernel(
    left_ref, corrected_ref, t_own_ref, gram_own_ref, t_ref, gram_ref, terms_ref, stack_ref
):
    t, gram = right_body(left_ref, corrected_ref, terms_ref, stack_ref)
    t_ref[0:40] = t_own_ref[...]
    t_ref[40:80] = t
    gram_ref[0] = gram_own_ref[...]
    gram_ref[1] = gram


def right_part(left, corrected, own=None):
    both = own is not None
    n = 2 if both else 1
    return pl.pallas_call(
        right_both_kernel if both else right_kernel,
        in_specs=vmem(4 if both else 2),
        out_specs=vmem(3),
        out_shape=[
            jax.ShapeDtypeStruct((40 * n, 128), jnp.float32),
            jax.ShapeDtypeStruct((2, RANK, RANK) if both else (RANK, RANK), jnp.float32),
            jax.ShapeDtypeStruct((6 * RANK, D), jnp.bfloat16),
        ],
        scratch_shapes=[pltpu.VMEM((RANK, D), jnp.float32)],
        compiler_params=pltpu.CompilerParams(vmem_limit_bytes=24 * MIB),
        cost_estimate=cost(2 * 256 * D * 96, 2 * ROWS * D + 16 * RANK * D),
        name="right",
    )(left, corrected, *(own or ()))


def inverse_kernel(gram_ref, inverse_ref):
    row = lax.broadcasted_iota(jnp.int32, (RANK, RANK), 0)
    col = lax.broadcasted_iota(jnp.int32, (RANK, RANK), 1)
    eye = jnp.where(row == col, 1.0, 0.0).astype(jnp.float32)
    a = jnp.concatenate([gram_ref[0], eye, gram_ref[1], eye], axis=1)
    rows = lax.broadcasted_iota(jnp.int32, a.shape, 0)
    first = lax.broadcasted_iota(jnp.int32, a.shape, 1) < 2 * RANK
    for base in range(0, RANK, 4):
        below, across = [], []
        for k in range(base, base + 4):
            left = jnp.broadcast_to(a[:, k : k + 1], a.shape)
            right = jnp.broadcast_to(a[:, 2 * RANK + k : 2 * RANK + k + 1], a.shape)
            below.append(jnp.where(first, left, right))
            across.append(a[k : k + 1, :])
        done = a
        for p in range(4):
            k = base + p
            scale = lax.rsqrt(below[p][k : k + 1, :])
            below[p] = below[p] * scale
            across[p] = across[p] * scale
            for q in range(p + 1, 4):
                factor = below[p][base + q : base + q + 1, :]
                below[q] = below[q] - below[p] * factor
                across[q] = across[q] - factor * across[p]
            a = a - below[p] * across[p]
            done = jnp.where(rows == k, across[p], done)
        a = jnp.where(rows >= base + 4, a, done)
    inverse_ref[0] = a[:, RANK : 2 * RANK]
    inverse_ref[1] = a[:, 3 * RANK : 4 * RANK]


def inverses(gram):
    return pl.pallas_call(
        inverse_kernel,
        in_specs=vmem(1),
        out_specs=pl.BlockSpec(memory_space=pltpu.VMEM),
        out_shape=jax.ShapeDtypeStruct((2, RANK, RANK), jnp.float32),
        compiler_params=pltpu.CompilerParams(vmem_limit_bytes=4 * MIB),
        cost_estimate=cost(10_000_000, 8_000_000),
        name="inverse",
    )(gram)


def final_kernel(
    core_ref,
    t0_ref,
    t1_ref,
    t2_ref,
    t3_ref,
    inverse_ref,
    terms_own_ref,
    terms_other_ref,
    corrected_own_ref,
    corrected_other_ref,
    update_ref,
    errors_ref,
    right_ref,
    update_at,
    errors_at,
    sems,
):
    high = functools.partial(
        lax.dot_general, precision=lax.Precision.HIGHEST, preferred_element_type=jnp.float32
    )
    nt = (((1,), (1,)), ((), ()))
    nn = (((1,), (0,)), ((), ()))
    core = core_ref[0]
    t = (t0_ref[...] + t1_ref[...]) + (t2_ref[...] + t3_ref[...])
    t = t * (1.0 / HOSTS)
    copies, rights = [], []
    for n in range(2):
        m = core if n == 0 else 1 - core
        terms_ref = (terms_own_ref, terms_other_ref)[n]
        corrected_ref = (corrected_own_ref, corrected_other_ref)[n]
        mine = t[40 * n : 40 * n + 40]
        mine = jnp.concatenate([mine[:, RANK * q : RANK * q + RANK] for q in range(4)], axis=0)
        inverse = inverse_ref[n]
        rights.append((m, mine, inverse))
        hi, mid, lo = split3(high(high(mine, inverse, nt), inverse, nn))
        w = jnp.concatenate([hi, hi, hi, mid, mid, lo], axis=1)
        for b in range(COL_BLOCKS):
            cols = slice(b * CHUNK_COLS, (b + 1) * CHUNK_COLS)
            recon = jnp.dot(w, terms_ref[:, cols], preferred_element_type=jnp.float32)
            update_at[n, b] = recon.astype(jnp.bfloat16)
            errors_at[n, b] = (corrected_ref[:, cols].astype(jnp.float32) - recon).astype(
                jnp.bfloat16
            )
            there = pl.ds(b * CHUNK_COLS, CHUNK_COLS)
            pair = (
                pltpu.make_async_copy(
                    update_at.at[n, b], update_ref.at[m, :, there], sems.at[n, b, 0]
                ),
                pltpu.make_async_copy(
                    errors_at.at[n, b], errors_ref.at[0, m, :, there], sems.at[n, b, 1]
                ),
            )
            for copy in pair:
                copy.start()
            copies.extend(pair)
    for m, mine, inverse in rights:
        right_ref[m] = high(inverse, mine, nt)
    for copy in copies:
        copy.wait()


def final_part(core, ts, inverse, terms_own, terms_other, corrected_own, corrected_other):
    hbm = pl.BlockSpec(memory_space=pltpu.HBM)
    return pl.pallas_call(
        final_kernel,
        in_specs=[pl.BlockSpec(memory_space=pltpu.SMEM)] + vmem(9),
        out_specs=[hbm, hbm, pl.BlockSpec(memory_space=pltpu.VMEM)],
        out_shape=[
            jax.ShapeDtypeStruct((2, ROWS, D), jnp.bfloat16),
            jax.ShapeDtypeStruct((1, 2, ROWS, D), jnp.bfloat16),
            jax.ShapeDtypeStruct((2, RANK, ROWS), jnp.float32),
        ],
        scratch_shapes=[
            pltpu.VMEM((2, COL_BLOCKS, ROWS, CHUNK_COLS), jnp.bfloat16),
            pltpu.VMEM((2, COL_BLOCKS, ROWS, CHUNK_COLS), jnp.bfloat16),
            pltpu.SemaphoreType.DMA((2, COL_BLOCKS, 2)),
        ],
        compiler_params=pltpu.CompilerParams(vmem_limit_bytes=24 * MIB),
        cost_estimate=cost(2 * 2 * ROWS * 192 * D, 16 * ROWS * D),
        name="final",
    )(core, *ts, inverse, terms_own, terms_other, corrected_own, corrected_other)


def on_device(grads, errors, basis_in):
    core = lax.rem(lax.axis_index("tp"), 2).astype(jnp.int32)
    grads, errors, basis = (
        pltpu.with_memory_space_constraint(a, pltpu.HBM)
        for a in (grads, errors, jnp.swapaxes(basis_in, 1, 2))
    )
    corrected_other, left_other = left_part((1 - core)[None], grads, errors, basis)
    with jax.named_scope("left_core_swap"):
        arrived = permute(left_other, CORE_SWAP)
    corrected_own, left_own = left_part(core[None], grads, errors, basis)
    with jax.named_scope("left_sum"):
        parts = exchange(left_own + arrived)
        part = add_up(parts)
        p2, p3, p1 = (permute(part, z_pairs(k)) for k in (2, 3, 1))
        part = (part + p1) + (p3 + p2)
        left_own = exchange(jnp.broadcast_to(part[None], (CHUNKS,) + part.shape))
        left_other = permute(left_own, CORE_SWAP)
    t_own, gram_own, terms_own = right_part(left_own, corrected_own)
    t, gram, terms_other = right_part(left_other, corrected_other, (t_own, gram_own))
    with jax.named_scope("right_sum"):
        t2, t3, t1 = (permute(t, first_pairs(k)) for k in (2, 3, 1))
        t = (t + t1) + (t3 + t2)
        t2, t3, t1 = (permute(t, second_pairs(k)) for k in (2, 3, 1))
    inverse = inverses(gram)
    update, new_errors, right = final_part(
        core[None], (t, t1, t3, t2), inverse, terms_own, terms_other, corrected_own, corrected_other
    )
    return update, new_errors, jnp.swapaxes(right, 1, 2)


def solution(mesh):
    return jax.shard_map(
        on_device,
        mesh=mesh,
        in_specs=(P("dp", None, "tp", None), P("dp", None, "tp", None), P(None, "tp", None)),
        out_specs=(P(None, "tp", None), P("dp", None, "tp", None), P(None, "tp", None)),
        check_vma=False,
    )
```

```python
import functools

import jax
import jax.numpy as jnp
from jax import lax
from jax.experimental import pallas as pl
from jax.experimental.pallas import tpu as pltpu
from jax.sharding import PartitionSpec as P

D = 5120
ROWS = 160
RANK = 32
HOSTS = 16
CHUNKS = 32
CHUNK_COLS = 640
COL_BLOCKS = D // CHUNK_COLS
AXES = ("dp", "tp")
MIB = 1 << 20


def device(x, y, z, c):
    return (y * 4 + x) * 16 + z * 2 + c


def everyone():
    return [(x, y, z, c) for y in range(4) for x in range(4) for z in range(8) for c in range(2)]


def pairs(move):
    return [(device(*at), device(*move(*at))) for at in everyone()]


CORE_SWAP = pairs(lambda x, y, z, c: (x, y, z, 1 - c))


def z_pairs(k):
    return pairs(lambda x, y, z, c: (x, y, z ^ (2 * k), c))


def first_pairs(k):
    return pairs(lambda x, y, z, c: (x ^ k, y, z, c) if c == 0 else (x, y ^ k, z, c))


def second_pairs(k):
    return pairs(lambda x, y, z, c: (x, y ^ k, z, c) if c == 0 else (x ^ k, y, z, c))


GROUPS = [
    [device(x, y, zz * 2 + k, c) for k in range(2) for y in range(4) for x in range(4)]
    for zz in range(4)
    for c in range(2)
]


def exchange(parts):
    return lax.all_to_all(parts, AXES, 0, 0, axis_index_groups=GROUPS, tiled=True)


def permute(a, perm):
    return lax.ppermute(a, AXES, perm)


def split3(a):
    hi = a.astype(jnp.bfloat16)
    rest = a - hi.astype(jnp.float32)
    mid = rest.astype(jnp.bfloat16)
    lo = (rest - mid.astype(jnp.float32)).astype(jnp.bfloat16)
    return hi, mid, lo


high = functools.partial(
    lax.dot_general, precision=lax.Precision.HIGHEST, preferred_element_type=jnp.float32
)


def cost(flops, nbytes):
    return pl.CostEstimate(flops=flops, bytes_accessed=nbytes, transcendentals=0)


def vmem(n):
    return [pl.BlockSpec(memory_space=pltpu.VMEM)] * n


def left_kernel(m_ref, grads_ref, errors_ref, basis_ref, corrected_ref, left_ref, *scratch):
    grads_at, errors_at, basis_at, sems, basis_sem = scratch
    m = m_ref[0]
    basis_copy = pltpu.make_async_copy(basis_ref.at[m], basis_at, basis_sem)
    basis_copy.start()
    copies = []
    for b in range(2):
        cols = pl.ds(b * (D // 2), D // 2)
        pair = (
            pltpu.make_async_copy(grads_ref.at[0, m, :, cols], grads_at.at[:, cols], sems.at[b, 0]),
            pltpu.make_async_copy(
                errors_ref.at[0, m, :, cols], errors_at.at[:, cols], sems.at[b, 1]
            ),
        )
        for copy in pair:
            copy.start()
        copies.append(pair)
    basis_copy.wait()
    basis = basis_at[...].astype(jnp.bfloat16)
    for b in range(COL_BLOCKS):
        if b % (COL_BLOCKS // 2) == 0:
            for copy in copies[b // (COL_BLOCKS // 2)]:
                copy.wait()
        cols = slice(b * CHUNK_COLS, (b + 1) * CHUNK_COLS)
        corrected = (
            grads_at[:, cols].astype(jnp.float32) + errors_at[:, cols].astype(jnp.float32)
        ).astype(jnp.bfloat16)
        corrected_ref[:, cols] = corrected
        left = jnp.dot(basis, corrected, preferred_element_type=jnp.float32)
        for g in range(4):
            left_ref[b * 4 + g] = left[8 * g : 8 * g + 8]


def left_part(m, grads, errors, basis):
    return pl.pallas_call(
        left_kernel,
        in_specs=[
            pl.BlockSpec(memory_space=pltpu.SMEM),
        ]
        + [pl.BlockSpec(memory_space=pltpu.HBM)] * 3,
        out_specs=vmem(2),
        out_shape=[
            jax.ShapeDtypeStruct((ROWS, D), jnp.bfloat16),
            jax.ShapeDtypeStruct((CHUNKS, 8, CHUNK_COLS), jnp.float32),
        ],
        scratch_shapes=[
            pltpu.VMEM((ROWS, D), jnp.bfloat16),
            pltpu.VMEM((ROWS, D), jnp.bfloat16),
            pltpu.VMEM((RANK, ROWS), jnp.float32),
            pltpu.SemaphoreType.DMA((2, 2)),
            pltpu.SemaphoreType.DMA(()),
        ],
        compiler_params=pltpu.CompilerParams(vmem_limit_bytes=16 * MIB),
        cost_estimate=cost(2 * ROWS * D * RANK, 6 * ROWS * D + 4 * RANK * D),
        name="left",
    )(m, grads, errors, basis)


def add_up_kernel(parts_ref, sum_ref):
    parts = [parts_ref[k] for k in range(CHUNKS)]
    while len(parts) > 1:
        parts = [parts[k] + parts[k + 1] for k in range(0, len(parts), 2)]
    sum_ref[...] = parts[0]


def add_up(parts):
    return pl.pallas_call(
        add_up_kernel,
        in_specs=vmem(1),
        out_specs=pl.BlockSpec(memory_space=pltpu.VMEM),
        out_shape=jax.ShapeDtypeStruct((8, CHUNK_COLS), jnp.float32),
        compiler_params=pltpu.CompilerParams(vmem_limit_bytes=4 * MIB),
        cost_estimate=cost(CHUNKS * 8 * CHUNK_COLS, 4 * CHUNKS * 8 * CHUNK_COLS),
        name="add_up",
    )(parts)


NT = (((1,), (1,)), ((), ()))


def right_body(left_ref, corrected_ref, terms_ref):
    for b in range(COL_BLOCKS):
        left = jnp.concatenate([left_ref[b * 4 + g] for g in range(4)], axis=0)
        for i, term in enumerate(split3(left)):
            terms_ref[i * RANK : (i + 1) * RANK, b * CHUNK_COLS : (b + 1) * CHUNK_COLS] = term
    t = lax.dot_general(
        corrected_ref[...], terms_ref[...], NT, preferred_element_type=jnp.float32
    )
    t = t[:, 0:RANK] + (t[:, RANK : 2 * RANK] + t[:, 2 * RANK : 3 * RANK])
    return jnp.concatenate([t[40 * i : 40 * i + 40] for i in range(4)], axis=1)


def gram_body(terms_ref):
    terms = terms_ref[...]
    g = lax.dot_general(terms, terms, NT, preferred_element_type=jnp.float32)
    rest = jnp.zeros((RANK, RANK), jnp.float32)
    for i in range(3):
        for j in range(3):
            if i + j > 0:
                rest = rest + g[i * RANK : (i + 1) * RANK, j * RANK : (j + 1) * RANK]
    return g[0:RANK, 0:RANK] + rest


def right_own_kernel(left_ref, corrected_ref, t_ref, terms_ref, gram_ref):
    t_ref[...] = right_body(left_ref, corrected_ref, terms_ref)
    gram_ref[...] = gram_body(terms_ref)


def right_other_kernel(left_ref, corrected_ref, t_own_ref, t_ref, terms_ref):
    t_ref[0:40] = t_own_ref[...]
    t_ref[40:80] = right_body(left_ref, corrected_ref, terms_ref)


def gram_kernel(terms_ref, gram_ref):
    gram_ref[...] = gram_body(terms_ref)


GRAM = jax.ShapeDtypeStruct((RANK, RANK), jnp.float32)


def right_part(left, corrected, t_own=None):
    own = t_own is None
    out_shape = [
        jax.ShapeDtypeStruct((40 if own else 80, 128), jnp.float32),
        jax.ShapeDtypeStruct((3 * RANK, D), jnp.bfloat16),
    ]
    if own:
        out_shape.append(GRAM)
    return pl.pallas_call(
        right_own_kernel if own else right_other_kernel,
        in_specs=vmem(2 if own else 3),
        out_specs=vmem(len(out_shape)),
        out_shape=out_shape,
        compiler_params=pltpu.CompilerParams(vmem_limit_bytes=16 * MIB),
        cost_estimate=cost(2 * 256 * D * 96, 2 * ROWS * D + 10 * RANK * D),
        name="right",
    )(left, corrected, *(() if own else (t_own,)))


def gram_part(terms):
    return pl.pallas_call(
        gram_kernel,
        in_specs=vmem(1),
        out_specs=pl.BlockSpec(memory_space=pltpu.VMEM),
        out_shape=GRAM,
        compiler_params=pltpu.CompilerParams(vmem_limit_bytes=4 * MIB),
        cost_estimate=cost(2 * 96 * D * 96, 6 * RANK * D),
        name="gram",
    )(terms)


def inverse_kernel(gram_own_ref, gram_other_ref, inverse_ref, gram_inverse_ref):
    row = lax.broadcasted_iota(jnp.int32, (RANK, RANK), 0)
    col = lax.broadcasted_iota(jnp.int32, (RANK, RANK), 1)
    eye = jnp.where(row == col, 1.0, 0.0).astype(jnp.float32)
    a = jnp.concatenate([gram_own_ref[...], eye, gram_other_ref[...], eye], axis=1)
    rows = lax.broadcasted_iota(jnp.int32, a.shape, 0)
    first = lax.broadcasted_iota(jnp.int32, a.shape, 1) < 2 * RANK
    for base in range(0, RANK, 4):
        below, across = [], []
        for k in range(base, base + 4):
            left = jnp.broadcast_to(a[:, k : k + 1], a.shape)
            right = jnp.broadcast_to(a[:, 2 * RANK + k : 2 * RANK + k + 1], a.shape)
            below.append(jnp.where(first, left, right))
            across.append(a[k : k + 1, :])
        done = a
        for p in range(4):
            k = base + p
            scale = lax.rsqrt(below[p][k : k + 1, :])
            below[p] = below[p] * scale
            across[p] = across[p] * scale
            for q in range(p + 1, 4):
                factor = below[p][base + q : base + q + 1, :]
                below[q] = below[q] - below[p] * factor
                across[q] = across[q] - factor * across[p]
            a = a - below[p] * across[p]
            done = jnp.where(rows == k, across[p], done)
        a = jnp.where(rows >= base + 4, a, done)
    for n in range(2):
        inverse = a[:, (2 * n + 1) * RANK : (2 * n + 2) * RANK]
        inverse_ref[n] = inverse
        gram_inverse_ref[n] = high(inverse, inverse, (((0,), (0,)), ((), ())))


def inverses(gram_own, gram_other):
    return pl.pallas_call(
        inverse_kernel,
        in_specs=vmem(2),
        out_specs=vmem(2),
        out_shape=[jax.ShapeDtypeStruct((2, RANK, RANK), jnp.float32)] * 2,
        compiler_params=pltpu.CompilerParams(vmem_limit_bytes=4 * MIB),
        cost_estimate=cost(10_000_000, 8_000_000),
        name="inverse",
    )(gram_own, gram_other)


def final_kernel(
    core_ref,
    t0_ref,
    t1_ref,
    t2_ref,
    t3_ref,
    inverse_ref,
    gram_inverse_ref,
    terms_own_ref,
    terms_other_ref,
    corrected_own_ref,
    corrected_other_ref,
    update_ref,
    errors_ref,
    right_ref,
    update_at,
    errors_at,
    sems,
):
    core = core_ref[0]
    t = (t0_ref[...] + t1_ref[...]) + (t2_ref[...] + t3_ref[...])
    t = t * (1.0 / HOSTS)
    copies, rights = [], []
    for n in range(2):
        m = core if n == 0 else 1 - core
        terms_ref = (terms_own_ref, terms_other_ref)[n]
        corrected_ref = (corrected_own_ref, corrected_other_ref)[n]
        mine = t[40 * n : 40 * n + 40]
        mine = jnp.concatenate([mine[:, RANK * q : RANK * q + RANK] for q in range(4)], axis=0)
        rights.append((m, mine, inverse_ref[n]))
        hi, mid, lo = split3(high(mine, gram_inverse_ref[n], (((1,), (0,)), ((), ()))))
        w = jnp.concatenate([hi, hi, hi, mid, mid, lo], axis=1)
        for b in range(COL_BLOCKS):
            cols = slice(b * CHUNK_COLS, (b + 1) * CHUNK_COLS)
            hi, mid, lo = (terms_ref[i * RANK : (i + 1) * RANK, cols] for i in range(3))
            terms = jnp.concatenate([hi, mid, lo, hi, mid, hi], axis=0)
            recon = jnp.dot(w, terms, preferred_element_type=jnp.float32)
            update_at[n, b] = recon.astype(jnp.bfloat16)
            errors_at[n, b] = (corrected_ref[:, cols].astype(jnp.float32) - recon).astype(
                jnp.bfloat16
            )
            there = pl.ds(b * CHUNK_COLS, CHUNK_COLS)
            pair = (
                pltpu.make_async_copy(
                    update_at.at[n, b], update_ref.at[m, :, there], sems.at[n, b, 0]
                ),
                pltpu.make_async_copy(
                    errors_at.at[n, b], errors_ref.at[0, m, :, there], sems.at[n, b, 1]
                ),
            )
            for copy in pair:
                copy.start()
            copies.extend(pair)
    for m, mine, inverse in rights:
        right_ref[m] = high(inverse, mine, NT)
    for copy in copies:
        copy.wait()


def final_part(core, ts, *rest):
    hbm = pl.BlockSpec(memory_space=pltpu.HBM)
    return pl.pallas_call(
        final_kernel,
        in_specs=[pl.BlockSpec(memory_space=pltpu.SMEM)] + vmem(10),
        out_specs=[hbm, hbm, pl.BlockSpec(memory_space=pltpu.VMEM)],
        out_shape=[
            jax.ShapeDtypeStruct((2, ROWS, D), jnp.bfloat16),
            jax.ShapeDtypeStruct((1, 2, ROWS, D), jnp.bfloat16),
            jax.ShapeDtypeStruct((2, RANK, ROWS), jnp.float32),
        ],
        scratch_shapes=[
            pltpu.VMEM((2, COL_BLOCKS, ROWS, CHUNK_COLS), jnp.bfloat16),
            pltpu.VMEM((2, COL_BLOCKS, ROWS, CHUNK_COLS), jnp.bfloat16),
            pltpu.SemaphoreType.DMA((2, COL_BLOCKS, 2)),
        ],
        compiler_params=pltpu.CompilerParams(vmem_limit_bytes=24 * MIB),
        cost_estimate=cost(2 * 2 * ROWS * 192 * D, 16 * ROWS * D),
        name="final",
    )(core, *ts, *rest)


def on_device(grads, errors, basis_in):
    core = lax.rem(lax.axis_index("tp"), 2).astype(jnp.int32)
    grads, errors, basis = (
        pltpu.with_memory_space_constraint(a, pltpu.HBM)
        for a in (grads, errors, jnp.swapaxes(basis_in, 1, 2))
    )
    corrected_other, left_other = left_part((1 - core)[None], grads, errors, basis)
    with jax.named_scope("left_core_swap"):
        arrived = permute(left_other, CORE_SWAP)
    corrected_own, left_own = left_part(core[None], grads, errors, basis)
    with jax.named_scope("left_sum"):
        parts = exchange(left_own + arrived)
        part = add_up(parts)
        p2, p3, p1 = (permute(part, z_pairs(k)) for k in (2, 3, 1))
        part = (part + p1) + (p3 + p2)
        left_own = exchange(jnp.broadcast_to(part[None], (CHUNKS,) + part.shape))
        left_other = permute(left_own, CORE_SWAP)
    t_own, terms_own, gram_own = right_part(left_own, corrected_own)
    t, terms_other = right_part(left_other, corrected_other, t_own)
    with jax.named_scope("right_sum"):
        t2, t3, t1 = (permute(t, first_pairs(k)) for k in (2, 3, 1))
        gram_other, t2 = lax.optimization_barrier((gram_part(terms_other), t2))
        t = (t + t1) + (t3 + t2)
        t2, t3, t1 = (permute(t, second_pairs(k)) for k in (2, 3, 1))
    inverse, gram_inverse = inverses(gram_own, gram_other)
    update, new_errors, right = final_part(
        core[None],
        (t, t1, t3, t2),
        inverse,
        gram_inverse,
        terms_own,
        terms_other,
        corrected_own,
        corrected_other,
    )
    return update, new_errors, jnp.swapaxes(right, 1, 2)


def solution(mesh):
    return jax.shard_map(
        on_device,
        mesh=mesh,
        in_specs=(P("dp", None, "tp", None), P("dp", None, "tp", None), P(None, "tp", None)),
        out_specs=(P(None, "tp", None), P("dp", None, "tp", None), P(None, "tp", None)),
        check_vma=False,
    )
```

```python
import functools

import jax
import jax.numpy as jnp
from jax import lax
from jax.experimental import pallas as pl
from jax.experimental.pallas import tpu as pltpu
from jax.sharding import PartitionSpec as P

D = 5120
ROWS = 160
RANK = 32
HOSTS = 16
CHUNKS = 32
CHUNK_COLS = 640
COL_BLOCKS = D // CHUNK_COLS
AXES = ("dp", "tp")
MIB = 1 << 20


def device(x, y, z, c):
    return (y * 4 + x) * 16 + z * 2 + c


def everyone():
    return [(x, y, z, c) for y in range(4) for x in range(4) for z in range(8) for c in range(2)]


def pairs(move):
    return [(device(*at), device(*move(*at))) for at in everyone()]


CORE_SWAP = pairs(lambda x, y, z, c: (x, y, z, 1 - c))


def z_pairs(planes):
    other = dict(planes + [(b, a) for a, b in planes])
    return pairs(lambda x, y, z, c: (x, y, other[z], c))


Z_NEAR = z_pairs([(1, 2), (3, 4), (5, 6), (7, 0)])
Z_FAR = z_pairs([(1, 6), (2, 5), (0, 3), (4, 7)])


def first_pairs(k):
    return pairs(lambda x, y, z, c: (x ^ k, y, z, c) if c == 0 else (x, y ^ k, z, c))


def second_pairs(k):
    return pairs(lambda x, y, z, c: (x, y ^ k, z, c) if c == 0 else (x ^ k, y, z, c))


GROUPS = [
    [device(x, y, zz * 2 + (k ^ (zz & 1)), c) for k in range(2) for y in range(4) for x in range(4)]
    for zz in range(4)
    for c in range(2)
]


def exchange(parts):
    return lax.all_to_all(parts, AXES, 0, 0, axis_index_groups=GROUPS, tiled=True)


def permute(a, perm):
    return lax.ppermute(a, AXES, perm)


def split3(a):
    hi = a.astype(jnp.bfloat16)
    rest = a - hi.astype(jnp.float32)
    mid = rest.astype(jnp.bfloat16)
    lo = (rest - mid.astype(jnp.float32)).astype(jnp.bfloat16)
    return hi, mid, lo


high = functools.partial(
    lax.dot_general, precision=lax.Precision.HIGHEST, preferred_element_type=jnp.float32
)


def cost(flops, nbytes):
    return pl.CostEstimate(flops=flops, bytes_accessed=nbytes, transcendentals=0)


def vmem(n):
    return [pl.BlockSpec(memory_space=pltpu.VMEM)] * n


def left_kernel(m_ref, grads_ref, errors_ref, basis_ref, corrected_ref, left_ref, *scratch):
    grads_at, errors_at, basis_at, sems, basis_sem = scratch
    m = m_ref[0]
    basis_copy = pltpu.make_async_copy(basis_ref.at[m], basis_at, basis_sem)
    basis_copy.start()
    copies = []
    for b in range(2):
        cols = pl.ds(b * (D // 2), D // 2)
        pair = (
            pltpu.make_async_copy(grads_ref.at[0, m, :, cols], grads_at.at[:, cols], sems.at[b, 0]),
            pltpu.make_async_copy(
                errors_ref.at[0, m, :, cols], errors_at.at[:, cols], sems.at[b, 1]
            ),
        )
        for copy in pair:
            copy.start()
        copies.append(pair)
    basis_copy.wait()
    basis = basis_at[...].astype(jnp.bfloat16)
    for b in range(COL_BLOCKS):
        if b % (COL_BLOCKS // 2) == 0:
            for copy in copies[b // (COL_BLOCKS // 2)]:
                copy.wait()
        cols = slice(b * CHUNK_COLS, (b + 1) * CHUNK_COLS)
        corrected = (
            grads_at[:, cols].astype(jnp.float32) + errors_at[:, cols].astype(jnp.float32)
        ).astype(jnp.bfloat16)
        corrected_ref[:, cols] = corrected
        left = jnp.dot(basis, corrected, preferred_element_type=jnp.float32)
        for g in range(4):
            left_ref[b * 4 + g] = left[8 * g : 8 * g + 8]


def left_part(m, grads, errors, basis):
    return pl.pallas_call(
        left_kernel,
        in_specs=[
            pl.BlockSpec(memory_space=pltpu.SMEM),
        ]
        + [pl.BlockSpec(memory_space=pltpu.HBM)] * 3,
        out_specs=vmem(2),
        out_shape=[
            jax.ShapeDtypeStruct((ROWS, D), jnp.bfloat16),
            jax.ShapeDtypeStruct((CHUNKS, 8, CHUNK_COLS), jnp.float32),
        ],
        scratch_shapes=[
            pltpu.VMEM((ROWS, D), jnp.bfloat16),
            pltpu.VMEM((ROWS, D), jnp.bfloat16),
            pltpu.VMEM((RANK, ROWS), jnp.float32),
            pltpu.SemaphoreType.DMA((2, 2)),
            pltpu.SemaphoreType.DMA(()),
        ],
        compiler_params=pltpu.CompilerParams(vmem_limit_bytes=16 * MIB),
        cost_estimate=cost(2 * ROWS * D * RANK, 6 * ROWS * D + 4 * RANK * D),
        name="left",
    )(m, grads, errors, basis)


def add_up_kernel(parts_ref, sum_ref):
    parts = [parts_ref[k] for k in range(CHUNKS)]
    while len(parts) > 1:
        parts = [parts[k] + parts[k + 1] for k in range(0, len(parts), 2)]
    sum_ref[...] = parts[0]


def add_up(parts):
    return pl.pallas_call(
        add_up_kernel,
        in_specs=vmem(1),
        out_specs=pl.BlockSpec(memory_space=pltpu.VMEM),
        out_shape=jax.ShapeDtypeStruct((8, CHUNK_COLS), jnp.float32),
        compiler_params=pltpu.CompilerParams(vmem_limit_bytes=4 * MIB),
        cost_estimate=cost(CHUNKS * 8 * CHUNK_COLS, 4 * CHUNKS * 8 * CHUNK_COLS),
        name="add_up",
    )(parts)


NT = (((1,), (1,)), ((), ()))


def right_body(left_ref, corrected_ref, terms_ref):
    for b in range(COL_BLOCKS):
        left = jnp.concatenate([left_ref[b * 4 + g] for g in range(4)], axis=0)
        for i, term in enumerate(split3(left)):
            terms_ref[i * RANK : (i + 1) * RANK, b * CHUNK_COLS : (b + 1) * CHUNK_COLS] = term
    t = lax.dot_general(
        corrected_ref[...], terms_ref[...], NT, preferred_element_type=jnp.float32
    )
    t = t[:, 0:RANK] + (t[:, RANK : 2 * RANK] + t[:, 2 * RANK : 3 * RANK])
    return jnp.concatenate([t[40 * i : 40 * i + 40] for i in range(4)], axis=1)


def gram_body(terms_ref):
    terms = terms_ref[...]
    g = lax.dot_general(terms, terms, NT, preferred_element_type=jnp.float32)
    rest = jnp.zeros((RANK, RANK), jnp.float32)
    for i in range(3):
        for j in range(3):
            if i + j > 0:
                rest = rest + g[i * RANK : (i + 1) * RANK, j * RANK : (j + 1) * RANK]
    return g[0:RANK, 0:RANK] + rest


def right_own_kernel(left_ref, corrected_ref, t_ref, terms_ref, gram_ref):
    t_ref[...] = right_body(left_ref, corrected_ref, terms_ref)
    gram_ref[...] = gram_body(terms_ref)


def right_other_kernel(left_ref, corrected_ref, t_own_ref, t_ref, terms_ref):
    t_ref[0:40] = t_own_ref[...]
    t_ref[40:80] = right_body(left_ref, corrected_ref, terms_ref)


def gram_kernel(terms_ref, gram_ref):
    gram_ref[...] = gram_body(terms_ref)


GRAM = jax.ShapeDtypeStruct((RANK, RANK), jnp.float32)


def right_part(left, corrected, t_own=None):
    own = t_own is None
    out_shape = [
        jax.ShapeDtypeStruct((40 if own else 80, 128), jnp.float32),
        jax.ShapeDtypeStruct((3 * RANK, D), jnp.bfloat16),
    ]
    if own:
        out_shape.append(GRAM)
    return pl.pallas_call(
        right_own_kernel if own else right_other_kernel,
        in_specs=vmem(2 if own else 3),
        out_specs=vmem(len(out_shape)),
        out_shape=out_shape,
        compiler_params=pltpu.CompilerParams(vmem_limit_bytes=16 * MIB),
        cost_estimate=cost(2 * 256 * D * 96, 2 * ROWS * D + 10 * RANK * D),
        name="right",
    )(left, corrected, *(() if own else (t_own,)))


def gram_part(terms):
    return pl.pallas_call(
        gram_kernel,
        in_specs=vmem(1),
        out_specs=pl.BlockSpec(memory_space=pltpu.VMEM),
        out_shape=GRAM,
        compiler_params=pltpu.CompilerParams(vmem_limit_bytes=4 * MIB),
        cost_estimate=cost(2 * 96 * D * 96, 6 * RANK * D),
        name="gram",
    )(terms)


def inverse_kernel(gram_own_ref, gram_other_ref, inverse_ref, gram_inverse_ref):
    row = lax.broadcasted_iota(jnp.int32, (RANK, RANK), 0)
    col = lax.broadcasted_iota(jnp.int32, (RANK, RANK), 1)
    eye = jnp.where(row == col, 1.0, 0.0).astype(jnp.float32)
    a = jnp.concatenate([gram_own_ref[...], eye, gram_other_ref[...], eye], axis=1)
    rows = lax.broadcasted_iota(jnp.int32, a.shape, 0)
    first = lax.broadcasted_iota(jnp.int32, a.shape, 1) < 2 * RANK
    for base in range(0, RANK, 4):
        below, across = [], []
        for k in range(base, base + 4):
            left = jnp.broadcast_to(a[:, k : k + 1], a.shape)
            right = jnp.broadcast_to(a[:, 2 * RANK + k : 2 * RANK + k + 1], a.shape)
            below.append(jnp.where(first, left, right))
            across.append(a[k : k + 1, :])
        done = a
        for p in range(4):
            k = base + p
            scale = lax.rsqrt(below[p][k : k + 1, :])
            below[p] = below[p] * scale
            across[p] = across[p] * scale
            for q in range(p + 1, 4):
                factor = below[p][base + q : base + q + 1, :]
                below[q] = below[q] - below[p] * factor
                across[q] = across[q] - factor * across[p]
            a = a - below[p] * across[p]
            done = jnp.where(rows == k, across[p], done)
        a = jnp.where(rows >= base + 4, a, done)
    for n in range(2):
        inverse = a[:, (2 * n + 1) * RANK : (2 * n + 2) * RANK]
        inverse_ref[n] = inverse
        gram_inverse_ref[n] = high(inverse, inverse, (((0,), (0,)), ((), ())))


def inverses(gram_own, gram_other):
    return pl.pallas_call(
        inverse_kernel,
        in_specs=vmem(2),
        out_specs=vmem(2),
        out_shape=[jax.ShapeDtypeStruct((2, RANK, RANK), jnp.float32)] * 2,
        compiler_params=pltpu.CompilerParams(vmem_limit_bytes=4 * MIB),
        cost_estimate=cost(10_000_000, 8_000_000),
        name="inverse",
    )(gram_own, gram_other)


def final_kernel(
    core_ref,
    t0_ref,
    t1_ref,
    t2_ref,
    t3_ref,
    inverse_ref,
    gram_inverse_ref,
    terms_own_ref,
    terms_other_ref,
    corrected_own_ref,
    corrected_other_ref,
    update_ref,
    errors_ref,
    right_ref,
    update_at,
    errors_at,
    sems,
):
    core = core_ref[0]
    t = (t0_ref[...] + t1_ref[...]) + (t2_ref[...] + t3_ref[...])
    t = t * (1.0 / HOSTS)
    copies, rights = [], []
    for n in range(2):
        m = core if n == 0 else 1 - core
        terms_ref = (terms_own_ref, terms_other_ref)[n]
        corrected_ref = (corrected_own_ref, corrected_other_ref)[n]
        mine = t[40 * n : 40 * n + 40]
        mine = jnp.concatenate([mine[:, RANK * q : RANK * q + RANK] for q in range(4)], axis=0)
        rights.append((m, mine, inverse_ref[n]))
        hi, mid, lo = split3(high(mine, gram_inverse_ref[n], (((1,), (0,)), ((), ()))))
        w = jnp.concatenate([hi, hi, hi, mid, mid, lo], axis=1)
        for b in range(COL_BLOCKS):
            cols = slice(b * CHUNK_COLS, (b + 1) * CHUNK_COLS)
            hi, mid, lo = (terms_ref[i * RANK : (i + 1) * RANK, cols] for i in range(3))
            terms = jnp.concatenate([hi, mid, lo, hi, mid, hi], axis=0)
            recon = jnp.dot(w, terms, preferred_element_type=jnp.float32)
            update_at[n, b] = recon.astype(jnp.bfloat16)
            errors_at[n, b] = (corrected_ref[:, cols].astype(jnp.float32) - recon).astype(
                jnp.bfloat16
            )
            there = pl.ds(b * CHUNK_COLS, CHUNK_COLS)
            pair = (
                pltpu.make_async_copy(
                    update_at.at[n, b], update_ref.at[m, :, there], sems.at[n, b, 0]
                ),
                pltpu.make_async_copy(
                    errors_at.at[n, b], errors_ref.at[0, m, :, there], sems.at[n, b, 1]
                ),
            )
            for copy in pair:
                copy.start()
            copies.extend(pair)
    for m, mine, inverse in rights:
        right_ref[m] = high(inverse, mine, NT)
    for copy in copies:
        copy.wait()


def final_part(core, ts, *rest):
    hbm = pl.BlockSpec(memory_space=pltpu.HBM)
    return pl.pallas_call(
        final_kernel,
        in_specs=[pl.BlockSpec(memory_space=pltpu.SMEM)] + vmem(10),
        out_specs=[hbm, hbm, pl.BlockSpec(memory_space=pltpu.VMEM)],
        out_shape=[
            jax.ShapeDtypeStruct((2, ROWS, D), jnp.bfloat16),
            jax.ShapeDtypeStruct((1, 2, ROWS, D), jnp.bfloat16),
            jax.ShapeDtypeStruct((2, RANK, ROWS), jnp.float32),
        ],
        scratch_shapes=[
            pltpu.VMEM((2, COL_BLOCKS, ROWS, CHUNK_COLS), jnp.bfloat16),
            pltpu.VMEM((2, COL_BLOCKS, ROWS, CHUNK_COLS), jnp.bfloat16),
            pltpu.SemaphoreType.DMA((2, COL_BLOCKS, 2)),
        ],
        compiler_params=pltpu.CompilerParams(vmem_limit_bytes=24 * MIB),
        cost_estimate=cost(2 * 2 * ROWS * 192 * D, 16 * ROWS * D),
        name="final",
    )(core, *ts, *rest)


def on_device(grads, errors, basis_in):
    core = lax.rem(lax.axis_index("tp"), 2).astype(jnp.int32)
    grads, errors, basis = (
        pltpu.with_memory_space_constraint(a, pltpu.HBM)
        for a in (grads, errors, jnp.swapaxes(basis_in, 1, 2))
    )
    corrected_other, left_other = left_part((1 - core)[None], grads, errors, basis)
    with jax.named_scope("left_core_swap"):
        arrived = permute(left_other, CORE_SWAP)
    corrected_own, left_own = left_part(core[None], grads, errors, basis)
    with jax.named_scope("left_sum"):
        parts = exchange(left_own + arrived)
        part = add_up(parts)
        part = part + permute(part, Z_NEAR)
        part = part + permute(part, Z_FAR)
        left_own = exchange(jnp.broadcast_to(part[None], (CHUNKS,) + part.shape))
        left_other = permute(left_own, CORE_SWAP)
    t_own, terms_own, gram_own = right_part(left_own, corrected_own)
    t, terms_other = right_part(left_other, corrected_other, t_own)
    with jax.named_scope("right_sum"):
        t2, t3, t1 = (permute(t, first_pairs(k)) for k in (2, 3, 1))
        gram_other, t2 = lax.optimization_barrier((gram_part(terms_other), t2))
        t = (t + t1) + (t3 + t2)
        t2, t3, t1 = (permute(t, second_pairs(k)) for k in (2, 3, 1))
    inverse, gram_inverse = inverses(gram_own, gram_other)
    update, new_errors, right = final_part(
        core[None],
        (t, t1, t3, t2),
        inverse,
        gram_inverse,
        terms_own,
        terms_other,
        corrected_own,
        corrected_other,
    )
    return update, new_errors, jnp.swapaxes(right, 1, 2)


def solution(mesh):
    return jax.shard_map(
        on_device,
        mesh=mesh,
        in_specs=(P("dp", None, "tp", None), P("dp", None, "tp", None), P(None, "tp", None)),
        out_specs=(P(None, "tp", None), P("dp", None, "tp", None), P(None, "tp", None)),
        check_vma=False,
    )
```

```python
import functools

import jax
import jax.numpy as jnp
from jax import lax
from jax.experimental import pallas as pl
from jax.experimental.pallas import tpu as pltpu
from jax.sharding import PartitionSpec as P

D = 5120
ROWS = 160
RANK = 32
HOSTS = 16
CHUNKS = 32
CHUNK_COLS = 640
COL_BLOCKS = D // CHUNK_COLS
AXES = ("dp", "tp")
MIB = 1 << 20


def device(x, y, z, c):
    return (y * 4 + x) * 16 + z * 2 + c


def everyone():
    return [(x, y, z, c) for y in range(4) for x in range(4) for z in range(8) for c in range(2)]


def pairs(move):
    return [(device(*at), device(*move(*at))) for at in everyone()]


CORE_SWAP = pairs(lambda x, y, z, c: (x, y, z, 1 - c))


def z_pairs(planes):
    other = dict(planes + [(b, a) for a, b in planes])
    return pairs(lambda x, y, z, c: (x, y, other[z], c))


Z_NEAR = z_pairs([(1, 2), (3, 4), (5, 6), (7, 0)])
Z_FAR = z_pairs([(1, 6), (2, 5), (0, 3), (4, 7)])


def first_pairs(k):
    return pairs(lambda x, y, z, c: (x ^ k, y, z, c) if c == 0 else (x, y ^ k, z, c))


def second_pairs(k):
    return pairs(lambda x, y, z, c: (x, y ^ k, z, c) if c == 0 else (x ^ k, y, z, c))


GROUPS = [
    [device(x, y, zz * 2 + (k ^ (zz & 1)), c) for k in range(2) for y in range(4) for x in range(4)]
    for zz in range(4)
    for c in range(2)
]


def exchange(parts):
    return lax.all_to_all(parts, AXES, 0, 0, axis_index_groups=GROUPS, tiled=True)


def permute(a, perm):
    return lax.ppermute(a, AXES, perm)


def split3(a):
    hi = a.astype(jnp.bfloat16)
    rest = a - hi.astype(jnp.float32)
    mid = rest.astype(jnp.bfloat16)
    lo = (rest - mid.astype(jnp.float32)).astype(jnp.bfloat16)
    return hi, mid, lo


high = functools.partial(
    lax.dot_general, precision=lax.Precision.HIGHEST, preferred_element_type=jnp.float32
)


def cost(flops, nbytes):
    return pl.CostEstimate(flops=flops, bytes_accessed=nbytes, transcendentals=0)


def vmem(n):
    return [pl.BlockSpec(memory_space=pltpu.VMEM)] * n


def left_kernel(m_ref, grads_ref, errors_ref, basis_ref, corrected_ref, left_ref, *scratch):
    grads_at, errors_at, basis_at, sems, basis_sem = scratch
    m = m_ref[0]
    basis_copy = pltpu.make_async_copy(basis_ref.at[m], basis_at, basis_sem)
    basis_copy.start()
    copies = []
    for b in range(2):
        cols = pl.ds(b * (D // 2), D // 2)
        pair = (
            pltpu.make_async_copy(grads_ref.at[0, m, :, cols], grads_at.at[:, cols], sems.at[b, 0]),
            pltpu.make_async_copy(
                errors_ref.at[0, m, :, cols], errors_at.at[:, cols], sems.at[b, 1]
            ),
        )
        for copy in pair:
            copy.start()
        copies.append(pair)
    basis_copy.wait()
    basis = basis_at[...].astype(jnp.bfloat16)
    for b in range(COL_BLOCKS):
        if b % (COL_BLOCKS // 2) == 0:
            for copy in copies[b // (COL_BLOCKS // 2)]:
                copy.wait()
        cols = slice(b * CHUNK_COLS, (b + 1) * CHUNK_COLS)
        corrected = (
            grads_at[:, cols].astype(jnp.float32) + errors_at[:, cols].astype(jnp.float32)
        ).astype(jnp.bfloat16)
        corrected_ref[:, cols] = corrected
        left = jnp.dot(basis, corrected, preferred_element_type=jnp.float32)
        for g in range(4):
            left_ref[b * 4 + g] = left[8 * g : 8 * g + 8]


def left_part(m, grads, errors, basis):
    return pl.pallas_call(
        left_kernel,
        in_specs=[
            pl.BlockSpec(memory_space=pltpu.SMEM),
        ]
        + [pl.BlockSpec(memory_space=pltpu.HBM)] * 3,
        out_specs=vmem(2),
        out_shape=[
            jax.ShapeDtypeStruct((ROWS, D), jnp.bfloat16),
            jax.ShapeDtypeStruct((CHUNKS, 8, CHUNK_COLS), jnp.float32),
        ],
        scratch_shapes=[
            pltpu.VMEM((ROWS, D), jnp.bfloat16),
            pltpu.VMEM((ROWS, D), jnp.bfloat16),
            pltpu.VMEM((RANK, ROWS), jnp.float32),
            pltpu.SemaphoreType.DMA((2, 2)),
            pltpu.SemaphoreType.DMA(()),
        ],
        compiler_params=pltpu.CompilerParams(vmem_limit_bytes=16 * MIB),
        cost_estimate=cost(2 * ROWS * D * RANK, 6 * ROWS * D + 4 * RANK * D),
        name="left",
    )(m, grads, errors, basis)


def add_up_kernel(parts_ref, sum_ref):
    parts = [parts_ref[k] for k in range(CHUNKS)]
    while len(parts) > 1:
        parts = [parts[k] + parts[k + 1] for k in range(0, len(parts), 2)]
    sum_ref[...] = parts[0]


def add_up(parts):
    return pl.pallas_call(
        add_up_kernel,
        in_specs=vmem(1),
        out_specs=pl.BlockSpec(memory_space=pltpu.VMEM),
        out_shape=jax.ShapeDtypeStruct((8, CHUNK_COLS), jnp.float32),
        compiler_params=pltpu.CompilerParams(vmem_limit_bytes=4 * MIB),
        cost_estimate=cost(CHUNKS * 8 * CHUNK_COLS, 4 * CHUNKS * 8 * CHUNK_COLS),
        name="add_up",
    )(parts)


NT = (((1,), (1,)), ((), ()))


def right_body(left_ref, corrected_ref, terms_ref):
    for b in range(COL_BLOCKS):
        left = jnp.concatenate([left_ref[b * 4 + g] for g in range(4)], axis=0)
        for i, term in enumerate(split3(left)):
            terms_ref[i * RANK : (i + 1) * RANK, b * CHUNK_COLS : (b + 1) * CHUNK_COLS] = term
    t = lax.dot_general(
        corrected_ref[...], terms_ref[...], NT, preferred_element_type=jnp.float32
    )
    t = t[:, 0:RANK] + (t[:, RANK : 2 * RANK] + t[:, 2 * RANK : 3 * RANK])
    return jnp.concatenate([t[40 * i : 40 * i + 40] for i in range(4)], axis=1)


def gram_body(terms_ref):
    terms = terms_ref[...]
    g = lax.dot_general(terms, terms, NT, preferred_element_type=jnp.float32)
    rest = jnp.zeros((RANK, RANK), jnp.float32)
    for i in range(3):
        for j in range(3):
            if i + j > 0:
                rest = rest + g[i * RANK : (i + 1) * RANK, j * RANK : (j + 1) * RANK]
    return g[0:RANK, 0:RANK] + rest


def right_own_kernel(left_ref, corrected_ref, t_ref, terms_ref, gram_ref):
    t_ref[...] = right_body(left_ref, corrected_ref, terms_ref)
    gram_ref[...] = gram_body(terms_ref)


def right_other_kernel(left_ref, corrected_ref, t_own_ref, t_ref, terms_ref):
    t_ref[0:40] = t_own_ref[...]
    t_ref[40:80] = right_body(left_ref, corrected_ref, terms_ref)


def gram_kernel(terms_ref, gram_ref):
    gram_ref[...] = gram_body(terms_ref)


GRAM = jax.ShapeDtypeStruct((RANK, RANK), jnp.float32)


def right_part(left, corrected, t_own=None):
    own = t_own is None
    out_shape = [
        jax.ShapeDtypeStruct((40 if own else 80, 128), jnp.float32),
        jax.ShapeDtypeStruct((3 * RANK, D), jnp.bfloat16),
    ]
    if own:
        out_shape.append(GRAM)
    return pl.pallas_call(
        right_own_kernel if own else right_other_kernel,
        in_specs=vmem(2 if own else 3),
        out_specs=vmem(len(out_shape)),
        out_shape=out_shape,
        compiler_params=pltpu.CompilerParams(vmem_limit_bytes=16 * MIB),
        cost_estimate=cost(2 * 256 * D * 96, 2 * ROWS * D + 10 * RANK * D),
        name="right",
    )(left, corrected, *(() if own else (t_own,)))


def gram_part(terms):
    return pl.pallas_call(
        gram_kernel,
        in_specs=vmem(1),
        out_specs=pl.BlockSpec(memory_space=pltpu.VMEM),
        out_shape=GRAM,
        compiler_params=pltpu.CompilerParams(vmem_limit_bytes=4 * MIB),
        cost_estimate=cost(2 * 96 * D * 96, 6 * RANK * D),
        name="gram",
    )(terms)


def inverse_kernel(gram_own_ref, gram_other_ref, inverse_ref, gram_inverse_ref):
    row = lax.broadcasted_iota(jnp.int32, (RANK, RANK), 0)
    col = lax.broadcasted_iota(jnp.int32, (RANK, RANK), 1)
    eye = jnp.where(row == col, 1.0, 0.0).astype(jnp.float32)
    a = jnp.concatenate([gram_own_ref[...], eye, gram_other_ref[...], eye], axis=1)
    rows = lax.broadcasted_iota(jnp.int32, a.shape, 0)
    first = lax.broadcasted_iota(jnp.int32, a.shape, 1) < 2 * RANK
    for base in range(0, RANK, 4):
        below, across = [], []
        for k in range(base, base + 4):
            left = jnp.broadcast_to(a[:, k : k + 1], a.shape)
            right = jnp.broadcast_to(a[:, 2 * RANK + k : 2 * RANK + k + 1], a.shape)
            below.append(jnp.where(first, left, right))
            across.append(a[k : k + 1, :])
        done = a
        for p in range(4):
            k = base + p
            scale = lax.rsqrt(below[p][k : k + 1, :])
            below[p] = below[p] * scale
            across[p] = across[p] * scale
            for q in range(p + 1, 4):
                factor = below[p][base + q : base + q + 1, :]
                below[q] = below[q] - below[p] * factor
                across[q] = across[q] - factor * across[p]
            a = a - below[p] * across[p]
            done = jnp.where(rows == k, across[p], done)
        a = jnp.where(rows >= base + 4, a, done)
    for n in range(2):
        inverse = a[:, (2 * n + 1) * RANK : (2 * n + 2) * RANK]
        inverse_ref[n] = inverse
        gram_inverse_ref[n] = high(inverse, inverse, (((0,), (0,)), ((), ())))


def inverses(gram_own, gram_other):
    return pl.pallas_call(
        inverse_kernel,
        in_specs=vmem(2),
        out_specs=vmem(2),
        out_shape=[jax.ShapeDtypeStruct((2, RANK, RANK), jnp.float32)] * 2,
        compiler_params=pltpu.CompilerParams(vmem_limit_bytes=4 * MIB),
        cost_estimate=cost(10_000_000, 8_000_000),
        name="inverse",
    )(gram_own, gram_other)


def final_kernel(
    core_ref,
    t0_ref,
    t1_ref,
    t2_ref,
    t3_ref,
    inverse_ref,
    gram_inverse_ref,
    terms_own_ref,
    terms_other_ref,
    corrected_own_ref,
    corrected_other_ref,
    update_ref,
    errors_ref,
    right_ref,
    update_at,
    errors_at,
    sems,
):
    core = core_ref[0]
    t = (t0_ref[...] + t1_ref[...]) + (t2_ref[...] + t3_ref[...])
    t = t * (1.0 / HOSTS)
    copies, rights, ws = [], [], []
    for n in range(2):
        m = core if n == 0 else 1 - core
        mine = t[40 * n : 40 * n + 40]
        mine = jnp.concatenate([mine[:, RANK * q : RANK * q + RANK] for q in range(4)], axis=0)
        rights.append((m, mine, inverse_ref[n]))
        hi, mid, lo = split3(high(mine, gram_inverse_ref[n], (((1,), (0,)), ((), ()))))
        ws.append(jnp.concatenate([hi, hi, hi, mid, mid, lo], axis=1))
    for n in range(2):
        m = core if n == 0 else 1 - core
        w = ws[n]
        terms_ref = (terms_own_ref, terms_other_ref)[n]
        corrected_ref = (corrected_own_ref, corrected_other_ref)[n]
        for b in range(COL_BLOCKS):
            cols = slice(b * CHUNK_COLS, (b + 1) * CHUNK_COLS)
            hi, mid, lo = (terms_ref[i * RANK : (i + 1) * RANK, cols] for i in range(3))
            terms = jnp.concatenate([hi, mid, lo, hi, mid, hi], axis=0)
            recon = jnp.dot(w, terms, preferred_element_type=jnp.float32)
            update_at[n, b] = recon.astype(jnp.bfloat16)
            errors_at[n, b] = (corrected_ref[:, cols].astype(jnp.float32) - recon).astype(
                jnp.bfloat16
            )
            there = pl.ds(b * CHUNK_COLS, CHUNK_COLS)
            pair = (
                pltpu.make_async_copy(
                    update_at.at[n, b], update_ref.at[m, :, there], sems.at[n, b, 0]
                ),
                pltpu.make_async_copy(
                    errors_at.at[n, b], errors_ref.at[0, m, :, there], sems.at[n, b, 1]
                ),
            )
            for copy in pair:
                copy.start()
            copies.extend(pair)
    for m, mine, inverse in rights:
        right_ref[m] = high(inverse, mine, NT)
    for copy in copies:
        copy.wait()


def final_part(core, ts, *rest):
    hbm = pl.BlockSpec(memory_space=pltpu.HBM)
    return pl.pallas_call(
        final_kernel,
        in_specs=[pl.BlockSpec(memory_space=pltpu.SMEM)] + vmem(10),
        out_specs=[hbm, hbm, pl.BlockSpec(memory_space=pltpu.VMEM)],
        out_shape=[
            jax.ShapeDtypeStruct((2, ROWS, D), jnp.bfloat16),
            jax.ShapeDtypeStruct((1, 2, ROWS, D), jnp.bfloat16),
            jax.ShapeDtypeStruct((2, RANK, ROWS), jnp.float32),
        ],
        scratch_shapes=[
            pltpu.VMEM((2, COL_BLOCKS, ROWS, CHUNK_COLS), jnp.bfloat16),
            pltpu.VMEM((2, COL_BLOCKS, ROWS, CHUNK_COLS), jnp.bfloat16),
            pltpu.SemaphoreType.DMA((2, COL_BLOCKS, 2)),
        ],
        compiler_params=pltpu.CompilerParams(vmem_limit_bytes=24 * MIB),
        cost_estimate=cost(2 * 2 * ROWS * 192 * D, 16 * ROWS * D),
        name="final",
    )(core, *ts, *rest)


def on_device(grads, errors, basis_in):
    core = lax.rem(lax.axis_index("tp"), 2).astype(jnp.int32)
    grads, errors, basis = (
        pltpu.with_memory_space_constraint(a, pltpu.HBM)
        for a in (grads, errors, jnp.swapaxes(basis_in, 1, 2))
    )
    corrected_other, left_other = left_part((1 - core)[None], grads, errors, basis)
    with jax.named_scope("left_core_swap"):
        arrived = permute(left_other, CORE_SWAP)
    corrected_own, left_own = left_part(core[None], grads, errors, basis)
    with jax.named_scope("left_sum"):
        parts = exchange(left_own + arrived)
        part = add_up(parts)
        part = part + permute(part, Z_FAR)
        part = part + permute(part, Z_NEAR)
        left_own = exchange(jnp.broadcast_to(part[None], (CHUNKS,) + part.shape))
        left_other = permute(left_own, CORE_SWAP)
    t_own, terms_own, gram_own = right_part(left_own, corrected_own)
    t, terms_other = right_part(left_other, corrected_other, t_own)
    with jax.named_scope("right_sum"):
        t2, t3, t1 = (permute(t, first_pairs(k)) for k in (2, 3, 1))
        gram_other, t2 = lax.optimization_barrier((gram_part(terms_other), t2))
        t = (t + t1) + (t3 + t2)
        t2, t3, t1 = (permute(t, second_pairs(k)) for k in (2, 3, 1))
    inverse, gram_inverse = inverses(gram_own, gram_other)
    update, new_errors, right = final_part(
        core[None],
        (t, t1, t3, t2),
        inverse,
        gram_inverse,
        terms_own,
        terms_other,
        corrected_own,
        corrected_other,
    )
    return update, new_errors, jnp.swapaxes(right, 1, 2)


def solution(mesh):
    return jax.shard_map(
        on_device,
        mesh=mesh,
        in_specs=(P("dp", None, "tp", None), P("dp", None, "tp", None), P(None, "tp", None)),
        out_specs=(P(None, "tp", None), P("dp", None, "tp", None), P(None, "tp", None)),
        check_vma=False,
    )
```

```python
import functools

import jax
import jax.numpy as jnp
from jax import lax
from jax.experimental import pallas as pl
from jax.experimental.pallas import tpu as pltpu
from jax.sharding import PartitionSpec as P

D = 5120
ROWS = 160
RANK = 32
HOSTS = 16
CHUNKS = 32
CHUNK_COLS = 640
COL_BLOCKS = D // CHUNK_COLS
AXES = ("dp", "tp")
MIB = 1 << 20


def device(x, y, z, c):
    return (y * 4 + x) * 16 + z * 2 + c


def everyone():
    return [(x, y, z, c) for y in range(4) for x in range(4) for z in range(8) for c in range(2)]


def pairs(move):
    return [(device(*at), device(*move(*at))) for at in everyone()]


CORE_SWAP = pairs(lambda x, y, z, c: (x, y, z, 1 - c))


def z_pairs(k):
    return pairs(lambda x, y, z, c: (x, y, z ^ k, c))


def first_pairs(k):
    return pairs(lambda x, y, z, c: (x ^ k, y, z, c) if c == 0 else (x, y ^ k, z, c))


def second_pairs(k):
    return pairs(lambda x, y, z, c: (x, y ^ k, z, c) if c == 0 else (x ^ k, y, z, c))


GROUPS = [
    [device(x, y, zz * 2 + k, c) for k in range(2) for y in range(4) for x in range(4)]
    for zz in range(4)
    for c in range(2)
]


def exchange(parts):
    return lax.all_to_all(parts, AXES, 0, 0, axis_index_groups=GROUPS, tiled=True)


def permute(a, perm):
    return lax.ppermute(a, AXES, perm)


def split3(a):
    hi = a.astype(jnp.bfloat16)
    rest = a - hi.astype(jnp.float32)
    mid = rest.astype(jnp.bfloat16)
    lo = (rest - mid.astype(jnp.float32)).astype(jnp.bfloat16)
    return hi, mid, lo


high = functools.partial(
    lax.dot_general, precision=lax.Precision.HIGHEST, preferred_element_type=jnp.float32
)


def cost(flops, nbytes):
    return pl.CostEstimate(flops=flops, bytes_accessed=nbytes, transcendentals=0)


def vmem(n):
    return [pl.BlockSpec(memory_space=pltpu.VMEM)] * n


def left_kernel(m_ref, grads_ref, errors_ref, basis_ref, corrected_ref, left_ref, *scratch):
    grads_at, errors_at, basis_at, sems, basis_sem = scratch
    m = m_ref[0]
    basis_copy = pltpu.make_async_copy(basis_ref.at[m], basis_at, basis_sem)
    basis_copy.start()
    copies = []
    for b in range(2):
        cols = pl.ds(b * (D // 2), D // 2)
        pair = (
            pltpu.make_async_copy(grads_ref.at[0, m, :, cols], grads_at.at[:, cols], sems.at[b, 0]),
            pltpu.make_async_copy(
                errors_ref.at[0, m, :, cols], errors_at.at[:, cols], sems.at[b, 1]
            ),
        )
        for copy in pair:
            copy.start()
        copies.append(pair)
    basis_copy.wait()
    basis = basis_at[...].astype(jnp.bfloat16)
    for b in range(COL_BLOCKS):
        if b % (COL_BLOCKS // 2) == 0:
            for copy in copies[b // (COL_BLOCKS // 2)]:
                copy.wait()
        cols = slice(b * CHUNK_COLS, (b + 1) * CHUNK_COLS)
        corrected = (
            grads_at[:, cols].astype(jnp.float32) + errors_at[:, cols].astype(jnp.float32)
        ).astype(jnp.bfloat16)
        corrected_ref[:, cols] = corrected
        left = jnp.dot(basis, corrected, preferred_element_type=jnp.float32)
        for g in range(4):
            left_ref[b * 4 + g] = left[8 * g : 8 * g + 8]


def left_part(m, grads, errors, basis):
    return pl.pallas_call(
        left_kernel,
        in_specs=[
            pl.BlockSpec(memory_space=pltpu.SMEM),
        ]
        + [pl.BlockSpec(memory_space=pltpu.HBM)] * 3,
        out_specs=vmem(2),
        out_shape=[
            jax.ShapeDtypeStruct((ROWS, D), jnp.bfloat16),
            jax.ShapeDtypeStruct((CHUNKS, 8, CHUNK_COLS), jnp.float32),
        ],
        scratch_shapes=[
            pltpu.VMEM((ROWS, D), jnp.bfloat16),
            pltpu.VMEM((ROWS, D), jnp.bfloat16),
            pltpu.VMEM((RANK, ROWS), jnp.float32),
            pltpu.SemaphoreType.DMA((2, 2)),
            pltpu.SemaphoreType.DMA(()),
        ],
        compiler_params=pltpu.CompilerParams(vmem_limit_bytes=16 * MIB),
        cost_estimate=cost(2 * ROWS * D * RANK, 6 * ROWS * D + 4 * RANK * D),
        name="left",
    )(m, grads, errors, basis)


def add_up_kernel(parts_ref, sum_ref):
    parts = [parts_ref[k] for k in range(CHUNKS)]
    while len(parts) > 1:
        parts = [parts[k] + parts[k + 1] for k in range(0, len(parts), 2)]
    sum_ref[...] = parts[0]


def add_up(parts):
    return pl.pallas_call(
        add_up_kernel,
        in_specs=vmem(1),
        out_specs=pl.BlockSpec(memory_space=pltpu.VMEM),
        out_shape=jax.ShapeDtypeStruct((8, CHUNK_COLS), jnp.float32),
        compiler_params=pltpu.CompilerParams(vmem_limit_bytes=4 * MIB),
        cost_estimate=cost(CHUNKS * 8 * CHUNK_COLS, 4 * CHUNKS * 8 * CHUNK_COLS),
        name="add_up",
    )(parts)


NT = (((1,), (1,)), ((), ()))


def right_body(left_ref, corrected_ref, terms_ref):
    for b in range(COL_BLOCKS):
        left = jnp.concatenate([left_ref[b * 4 + g] for g in range(4)], axis=0)
        for i, term in enumerate(split3(left)):
            terms_ref[i * RANK : (i + 1) * RANK, b * CHUNK_COLS : (b + 1) * CHUNK_COLS] = term
    t = lax.dot_general(
        corrected_ref[...], terms_ref[...], NT, preferred_element_type=jnp.float32
    )
    t = t[:, 0:RANK] + (t[:, RANK : 2 * RANK] + t[:, 2 * RANK : 3 * RANK])
    return jnp.concatenate([t[40 * i : 40 * i + 40] for i in range(4)], axis=1)


def gram_body(terms_ref):
    terms = terms_ref[...]
    g = lax.dot_general(terms, terms, NT, preferred_element_type=jnp.float32)
    rest = jnp.zeros((RANK, RANK), jnp.float32)
    for i in range(3):
        for j in range(3):
            if i + j > 0:
                rest = rest + g[i * RANK : (i + 1) * RANK, j * RANK : (j + 1) * RANK]
    return g[0:RANK, 0:RANK] + rest


def right_own_kernel(left_ref, corrected_ref, t_ref, terms_ref, gram_ref):
    t_ref[...] = right_body(left_ref, corrected_ref, terms_ref)
    gram_ref[...] = gram_body(terms_ref)


def right_other_kernel(left_ref, corrected_ref, t_own_ref, t_ref, terms_ref):
    t_ref[0:40] = t_own_ref[...]
    t_ref[40:80] = right_body(left_ref, corrected_ref, terms_ref)


def gram_kernel(terms_ref, gram_ref):
    gram_ref[...] = gram_body(terms_ref)


GRAM = jax.ShapeDtypeStruct((RANK, RANK), jnp.float32)


def right_part(left, corrected, t_own=None):
    own = t_own is None
    out_shape = [
        jax.ShapeDtypeStruct((40 if own else 80, 128), jnp.float32),
        jax.ShapeDtypeStruct((3 * RANK, D), jnp.bfloat16),
    ]
    if own:
        out_shape.append(GRAM)
    return pl.pallas_call(
        right_own_kernel if own else right_other_kernel,
        in_specs=vmem(2 if own else 3),
        out_specs=vmem(len(out_shape)),
        out_shape=out_shape,
        compiler_params=pltpu.CompilerParams(vmem_limit_bytes=16 * MIB),
        cost_estimate=cost(2 * 256 * D * 96, 2 * ROWS * D + 10 * RANK * D),
        name="right",
    )(left, corrected, *(() if own else (t_own,)))


def gram_part(terms):
    return pl.pallas_call(
        gram_kernel,
        in_specs=vmem(1),
        out_specs=pl.BlockSpec(memory_space=pltpu.VMEM),
        out_shape=GRAM,
        compiler_params=pltpu.CompilerParams(vmem_limit_bytes=4 * MIB),
        cost_estimate=cost(2 * 96 * D * 96, 6 * RANK * D),
        name="gram",
    )(terms)


def inverse_kernel(gram_own_ref, gram_other_ref, inverse_ref, gram_inverse_ref):
    row = lax.broadcasted_iota(jnp.int32, (RANK, RANK), 0)
    col = lax.broadcasted_iota(jnp.int32, (RANK, RANK), 1)
    eye = jnp.where(row == col, 1.0, 0.0).astype(jnp.float32)
    a = jnp.concatenate([gram_own_ref[...], eye, gram_other_ref[...], eye], axis=1)
    rows = lax.broadcasted_iota(jnp.int32, a.shape, 0)
    first = lax.broadcasted_iota(jnp.int32, a.shape, 1) < 2 * RANK
    for base in range(0, RANK, 4):
        below, across = [], []
        for k in range(base, base + 4):
            left = jnp.broadcast_to(a[:, k : k + 1], a.shape)
            right = jnp.broadcast_to(a[:, 2 * RANK + k : 2 * RANK + k + 1], a.shape)
            below.append(jnp.where(first, left, right))
            across.append(a[k : k + 1, :])
        done = a
        for p in range(4):
            k = base + p
            scale = lax.rsqrt(below[p][k : k + 1, :])
            below[p] = below[p] * scale
            across[p] = across[p] * scale
            for q in range(p + 1, 4):
                factor = below[p][base + q : base + q + 1, :]
                below[q] = below[q] - below[p] * factor
                across[q] = across[q] - factor * across[p]
            a = a - below[p] * across[p]
            done = jnp.where(rows == k, across[p], done)
        a = jnp.where(rows >= base + 4, a, done)
    for n in range(2):
        inverse = a[:, (2 * n + 1) * RANK : (2 * n + 2) * RANK]
        inverse_ref[n] = inverse
        gram_inverse_ref[n] = high(inverse, inverse, (((0,), (0,)), ((), ())))


def inverses(gram_own, gram_other):
    return pl.pallas_call(
        inverse_kernel,
        in_specs=vmem(2),
        out_specs=vmem(2),
        out_shape=[jax.ShapeDtypeStruct((2, RANK, RANK), jnp.float32)] * 2,
        compiler_params=pltpu.CompilerParams(vmem_limit_bytes=4 * MIB),
        cost_estimate=cost(10_000_000, 8_000_000),
        name="inverse",
    )(gram_own, gram_other)


def final_kernel(
    core_ref,
    t0_ref,
    t1_ref,
    t2_ref,
    t3_ref,
    inverse_ref,
    gram_inverse_ref,
    terms_own_ref,
    terms_other_ref,
    corrected_own_ref,
    corrected_other_ref,
    update_ref,
    errors_ref,
    right_ref,
    update_at,
    errors_at,
    sems,
):
    core = core_ref[0]
    t = (t0_ref[...] + t1_ref[...]) + (t2_ref[...] + t3_ref[...])
    t = t * (1.0 / HOSTS)
    copies, rights, ws = [], [], []
    for n in range(2):
        m = core if n == 0 else 1 - core
        mine = t[40 * n : 40 * n + 40]
        mine = jnp.concatenate([mine[:, RANK * q : RANK * q + RANK] for q in range(4)], axis=0)
        rights.append((m, mine, inverse_ref[n]))
        hi, mid, lo = split3(high(mine, gram_inverse_ref[n], (((1,), (0,)), ((), ()))))
        ws.append(jnp.concatenate([hi, hi, hi, mid, mid, lo], axis=1))
    for n in range(2):
        m = core if n == 0 else 1 - core
        w = ws[n]
        terms_ref = (terms_own_ref, terms_other_ref)[n]
        corrected_ref = (corrected_own_ref, corrected_other_ref)[n]
        for b in range(COL_BLOCKS):
            cols = slice(b * CHUNK_COLS, (b + 1) * CHUNK_COLS)
            hi, mid, lo = (terms_ref[i * RANK : (i + 1) * RANK, cols] for i in range(3))
            terms = jnp.concatenate([hi, mid, lo, hi, mid, hi], axis=0)
            recon = jnp.dot(w, terms, preferred_element_type=jnp.float32)
            update_at[n, b] = recon.astype(jnp.bfloat16)
            errors_at[n, b] = (corrected_ref[:, cols].astype(jnp.float32) - recon).astype(
                jnp.bfloat16
            )
            there = pl.ds(b * CHUNK_COLS, CHUNK_COLS)
            pair = (
                pltpu.make_async_copy(
                    update_at.at[n, b], update_ref.at[m, :, there], sems.at[n, b, 0]
                ),
                pltpu.make_async_copy(
                    errors_at.at[n, b], errors_ref.at[0, m, :, there], sems.at[n, b, 1]
                ),
            )
            for copy in pair:
                copy.start()
            copies.extend(pair)
    for m, mine, inverse in rights:
        right_ref[m] = high(inverse, mine, NT)
    for copy in copies:
        copy.wait()


def final_part(core, ts, *rest):
    hbm = pl.BlockSpec(memory_space=pltpu.HBM)
    return pl.pallas_call(
        final_kernel,
        in_specs=[pl.BlockSpec(memory_space=pltpu.SMEM)] + vmem(10),
        out_specs=[hbm, hbm, pl.BlockSpec(memory_space=pltpu.VMEM)],
        out_shape=[
            jax.ShapeDtypeStruct((2, ROWS, D), jnp.bfloat16),
            jax.ShapeDtypeStruct((1, 2, ROWS, D), jnp.bfloat16),
            jax.ShapeDtypeStruct((2, RANK, ROWS), jnp.float32),
        ],
        scratch_shapes=[
            pltpu.VMEM((2, COL_BLOCKS, ROWS, CHUNK_COLS), jnp.bfloat16),
            pltpu.VMEM((2, COL_BLOCKS, ROWS, CHUNK_COLS), jnp.bfloat16),
            pltpu.SemaphoreType.DMA((2, COL_BLOCKS, 2)),
        ],
        compiler_params=pltpu.CompilerParams(vmem_limit_bytes=24 * MIB),
        cost_estimate=cost(2 * 2 * ROWS * 192 * D, 16 * ROWS * D),
        name="final",
    )(core, *ts, *rest)


def on_device(grads, errors, basis_in):
    core = lax.rem(lax.axis_index("tp"), 2).astype(jnp.int32)
    grads, errors, basis = (
        pltpu.with_memory_space_constraint(a, pltpu.HBM)
        for a in (grads, errors, jnp.swapaxes(basis_in, 1, 2))
    )
    corrected_other, left_other = left_part((1 - core)[None], grads, errors, basis)
    with jax.named_scope("left_core_swap"):
        arrived = permute(left_other, CORE_SWAP)
    corrected_own, left_own = left_part(core[None], grads, errors, basis)
    with jax.named_scope("left_sum"):
        parts = exchange(left_own + arrived)
        part = add_up(parts)
        part = part + permute(part, z_pairs(2))
        part = part + permute(part, z_pairs(6))
        left_own = exchange(jnp.broadcast_to(part[None], (CHUNKS,) + part.shape))
        left_other = permute(left_own, CORE_SWAP)
    t_own, terms_own, gram_own = right_part(left_own, corrected_own)
    t, terms_other = right_part(left_other, corrected_other, t_own)
    with jax.named_scope("right_sum"):
        t2, t3, t1 = (permute(t, first_pairs(k)) for k in (2, 3, 1))
        gram_other, t2 = lax.optimization_barrier((gram_part(terms_other), t2))
        t = (t + t1) + (t3 + t2)
        t2, t3, t1 = (permute(t, second_pairs(k)) for k in (2, 3, 1))
    inverse, gram_inverse = inverses(gram_own, gram_other)
    update, new_errors, right = final_part(
        core[None],
        (t, t1, t3, t2),
        inverse,
        gram_inverse,
        terms_own,
        terms_other,
        corrected_own,
        corrected_other,
    )
    return update, new_errors, jnp.swapaxes(right, 1, 2)


def solution(mesh):
    return jax.shard_map(
        on_device,
        mesh=mesh,
        in_specs=(P("dp", None, "tp", None), P("dp", None, "tp", None), P(None, "tp", None)),
        out_specs=(P(None, "tp", None), P("dp", None, "tp", None), P(None, "tp", None)),
        check_vma=False,
    )
```

```python
import functools

import jax
import jax.numpy as jnp
from jax import lax
from jax.experimental import pallas as pl
from jax.experimental.pallas import tpu as pltpu
from jax.sharding import PartitionSpec as P

D = 5120
ROWS = 160
RANK = 32
HOSTS = 16
CHUNKS = 32
CHUNK_COLS = 640
COL_BLOCKS = D // CHUNK_COLS
AXES = ("dp", "tp")
MIB = 1 << 20


def device(x, y, z, c):
    return (y * 4 + x) * 16 + z * 2 + c


def everyone():
    return [(x, y, z, c) for y in range(4) for x in range(4) for z in range(8) for c in range(2)]


def pairs(move):
    return [(device(*at), device(*move(*at))) for at in everyone()]


CORE_SWAP = pairs(lambda x, y, z, c: (x, y, z, 1 - c))


def z_pairs(k):
    return pairs(lambda x, y, z, c: (x, y, z ^ k, c))


def first_pairs(k):
    return pairs(lambda x, y, z, c: (x ^ k, y, z, c) if c == 0 else (x, y ^ k, z, c))


def second_pairs(k):
    return pairs(lambda x, y, z, c: (x, y ^ k, z, c) if c == 0 else (x ^ k, y, z, c))


GROUPS = [
    [device(x, y, zz * 2 + k, c) for k in range(2) for y in range(4) for x in range(4)]
    for zz in range(4)
    for c in range(2)
]


def exchange(parts):
    return lax.all_to_all(parts, AXES, 0, 0, axis_index_groups=GROUPS, tiled=True)


def permute(a, perm):
    return lax.ppermute(a, AXES, perm)


def split3(a):
    hi = a.astype(jnp.bfloat16)
    rest = a - hi.astype(jnp.float32)
    mid = rest.astype(jnp.bfloat16)
    lo = (rest - mid.astype(jnp.float32)).astype(jnp.bfloat16)
    return hi, mid, lo


high = functools.partial(
    lax.dot_general, precision=lax.Precision.HIGHEST, preferred_element_type=jnp.float32
)


def cost(flops, nbytes):
    return pl.CostEstimate(flops=flops, bytes_accessed=nbytes, transcendentals=0)


def vmem(n):
    return [pl.BlockSpec(memory_space=pltpu.VMEM)] * n


def left_kernel(m_ref, grads_ref, errors_ref, basis_ref, corrected_ref, left_ref, *scratch):
    grads_at, errors_at, basis_at, sems, basis_sem = scratch
    m = m_ref[0]
    basis_copy = pltpu.make_async_copy(basis_ref.at[m], basis_at, basis_sem)
    basis_copy.start()
    copies = []
    for b, (at, width) in enumerate(((0, 3200), (3200, 1920))):
        cols = pl.ds(at, width)
        pair = (
            pltpu.make_async_copy(grads_ref.at[0, m, :, cols], grads_at.at[:, cols], sems.at[b, 0]),
            pltpu.make_async_copy(
                errors_ref.at[0, m, :, cols], errors_at.at[:, cols], sems.at[b, 1]
            ),
        )
        for copy in pair:
            copy.start()
        copies.append(pair)
    basis_copy.wait()
    basis = basis_at[...].astype(jnp.bfloat16)
    for b in range(COL_BLOCKS):
        if b in (0, 5):
            for copy in copies[b // 5]:
                copy.wait()
        cols = slice(b * CHUNK_COLS, (b + 1) * CHUNK_COLS)
        corrected = (
            grads_at[:, cols].astype(jnp.float32) + errors_at[:, cols].astype(jnp.float32)
        ).astype(jnp.bfloat16)
        corrected_ref[:, cols] = corrected
        left = jnp.dot(basis, corrected, preferred_element_type=jnp.float32)
        for g in range(4):
            left_ref[b * 4 + g] = left[8 * g : 8 * g + 8]


def left_part(m, grads, errors, basis):
    return pl.pallas_call(
        left_kernel,
        in_specs=[
            pl.BlockSpec(memory_space=pltpu.SMEM),
        ]
        + [pl.BlockSpec(memory_space=pltpu.HBM)] * 3,
        out_specs=vmem(2),
        out_shape=[
            jax.ShapeDtypeStruct((ROWS, D), jnp.bfloat16),
            jax.ShapeDtypeStruct((CHUNKS, 8, CHUNK_COLS), jnp.float32),
        ],
        scratch_shapes=[
            pltpu.VMEM((ROWS, D), jnp.bfloat16),
            pltpu.VMEM((ROWS, D), jnp.bfloat16),
            pltpu.VMEM((RANK, ROWS), jnp.float32),
            pltpu.SemaphoreType.DMA((2, 2)),
            pltpu.SemaphoreType.DMA(()),
        ],
        compiler_params=pltpu.CompilerParams(vmem_limit_bytes=16 * MIB),
        cost_estimate=cost(2 * ROWS * D * RANK, 6 * ROWS * D + 4 * RANK * D),
        name="left",
    )(m, grads, errors, basis)


def add_up_kernel(parts_ref, sum_ref):
    parts = [parts_ref[k] for k in range(CHUNKS)]
    while len(parts) > 1:
        parts = [parts[k] + parts[k + 1] for k in range(0, len(parts), 2)]
    sum_ref[...] = parts[0]


def add_up(parts):
    return pl.pallas_call(
        add_up_kernel,
        in_specs=vmem(1),
        out_specs=pl.BlockSpec(memory_space=pltpu.VMEM),
        out_shape=jax.ShapeDtypeStruct((8, CHUNK_COLS), jnp.float32),
        compiler_params=pltpu.CompilerParams(vmem_limit_bytes=4 * MIB),
        cost_estimate=cost(CHUNKS * 8 * CHUNK_COLS, 4 * CHUNKS * 8 * CHUNK_COLS),
        name="add_up",
    )(parts)


NT = (((1,), (1,)), ((), ()))


def right_body(left_ref, corrected_ref, terms_ref):
    for b in range(COL_BLOCKS):
        left = jnp.concatenate([left_ref[b * 4 + g] for g in range(4)], axis=0)
        for i, term in enumerate(split3(left)):
            terms_ref[i * RANK : (i + 1) * RANK, b * CHUNK_COLS : (b + 1) * CHUNK_COLS] = term
    t = lax.dot_general(
        corrected_ref[...], terms_ref[...], NT, preferred_element_type=jnp.float32
    )
    t = t[:, 0:RANK] + (t[:, RANK : 2 * RANK] + t[:, 2 * RANK : 3 * RANK])
    return jnp.concatenate([t[40 * i : 40 * i + 40] for i in range(4)], axis=1)


def gram_body(terms_ref):
    terms = terms_ref[...]
    g = lax.dot_general(terms, terms, NT, preferred_element_type=jnp.float32)
    rest = jnp.zeros((RANK, RANK), jnp.float32)
    for i in range(3):
        for j in range(3):
            if i + j > 0:
                rest = rest + g[i * RANK : (i + 1) * RANK, j * RANK : (j + 1) * RANK]
    return g[0:RANK, 0:RANK] + rest


def right_own_kernel(left_ref, corrected_ref, t_ref, terms_ref, gram_ref):
    t_ref[...] = right_body(left_ref, corrected_ref, terms_ref)
    gram_ref[...] = gram_body(terms_ref)


def right_other_kernel(left_ref, corrected_ref, t_own_ref, t_ref, terms_ref):
    t_ref[0:40] = t_own_ref[...]
    t_ref[40:80] = right_body(left_ref, corrected_ref, terms_ref)


def gram_kernel(terms_ref, gram_ref):
    gram_ref[...] = gram_body(terms_ref)


GRAM = jax.ShapeDtypeStruct((RANK, RANK), jnp.float32)


def right_part(left, corrected, t_own=None):
    own = t_own is None
    out_shape = [
        jax.ShapeDtypeStruct((40 if own else 80, 128), jnp.float32),
        jax.ShapeDtypeStruct((3 * RANK, D), jnp.bfloat16),
    ]
    if own:
        out_shape.append(GRAM)
    return pl.pallas_call(
        right_own_kernel if own else right_other_kernel,
        in_specs=vmem(2 if own else 3),
        out_specs=vmem(len(out_shape)),
        out_shape=out_shape,
        compiler_params=pltpu.CompilerParams(vmem_limit_bytes=16 * MIB),
        cost_estimate=cost(2 * 256 * D * 96, 2 * ROWS * D + 10 * RANK * D),
        name="right",
    )(left, corrected, *(() if own else (t_own,)))


def gram_part(terms):
    return pl.pallas_call(
        gram_kernel,
        in_specs=vmem(1),
        out_specs=pl.BlockSpec(memory_space=pltpu.VMEM),
        out_shape=GRAM,
        compiler_params=pltpu.CompilerParams(vmem_limit_bytes=4 * MIB),
        cost_estimate=cost(2 * 96 * D * 96, 6 * RANK * D),
        name="gram",
    )(terms)


def inverse_kernel(gram_own_ref, gram_other_ref, inverse_ref, gram_inverse_ref):
    row = lax.broadcasted_iota(jnp.int32, (RANK, RANK), 0)
    col = lax.broadcasted_iota(jnp.int32, (RANK, RANK), 1)
    eye = jnp.where(row == col, 1.0, 0.0).astype(jnp.float32)
    a = jnp.concatenate([gram_own_ref[...], eye, gram_other_ref[...], eye], axis=1)
    rows = lax.broadcasted_iota(jnp.int32, a.shape, 0)
    first = lax.broadcasted_iota(jnp.int32, a.shape, 1) < 2 * RANK
    for base in range(0, RANK, 4):
        below, across = [], []
        for k in range(base, base + 4):
            left = jnp.broadcast_to(a[:, k : k + 1], a.shape)
            right = jnp.broadcast_to(a[:, 2 * RANK + k : 2 * RANK + k + 1], a.shape)
            below.append(jnp.where(first, left, right))
            across.append(a[k : k + 1, :])
        done = a
        for p in range(4):
            k = base + p
            scale = lax.rsqrt(below[p][k : k + 1, :])
            below[p] = below[p] * scale
            across[p] = across[p] * scale
            for q in range(p + 1, 4):
                factor = below[p][base + q : base + q + 1, :]
                below[q] = below[q] - below[p] * factor
                across[q] = across[q] - factor * across[p]
            a = a - below[p] * across[p]
            done = jnp.where(rows == k, across[p], done)
        a = jnp.where(rows >= base + 4, a, done)
    for n in range(2):
        inverse = a[:, (2 * n + 1) * RANK : (2 * n + 2) * RANK]
        inverse_ref[n] = inverse
        gram_inverse_ref[n] = high(inverse, inverse, (((0,), (0,)), ((), ())))


def inverses(gram_own, gram_other):
    return pl.pallas_call(
        inverse_kernel,
        in_specs=vmem(2),
        out_specs=vmem(2),
        out_shape=[jax.ShapeDtypeStruct((2, RANK, RANK), jnp.float32)] * 2,
        compiler_params=pltpu.CompilerParams(vmem_limit_bytes=4 * MIB),
        cost_estimate=cost(10_000_000, 8_000_000),
        name="inverse",
    )(gram_own, gram_other)


def final_kernel(
    core_ref,
    t0_ref,
    t1_ref,
    t2_ref,
    t3_ref,
    inverse_ref,
    gram_inverse_ref,
    terms_own_ref,
    terms_other_ref,
    corrected_own_ref,
    corrected_other_ref,
    update_ref,
    errors_ref,
    right_ref,
    update_at,
    errors_at,
    sems,
):
    core = core_ref[0]
    t = (t0_ref[...] + t1_ref[...]) + (t2_ref[...] + t3_ref[...])
    t = t * (1.0 / HOSTS)
    copies, rights, ws = [], [], []
    for n in range(2):
        m = core if n == 0 else 1 - core
        mine = t[40 * n : 40 * n + 40]
        mine = jnp.concatenate([mine[:, RANK * q : RANK * q + RANK] for q in range(4)], axis=0)
        rights.append((m, mine, inverse_ref[n]))
        hi, mid, lo = split3(high(mine, gram_inverse_ref[n], (((1,), (0,)), ((), ()))))
        ws.append(jnp.concatenate([hi, hi, hi, mid, mid, lo], axis=1))
    for n in range(2):
        m = core if n == 0 else 1 - core
        w = ws[n]
        terms_ref = (terms_own_ref, terms_other_ref)[n]
        corrected_ref = (corrected_own_ref, corrected_other_ref)[n]
        for b in range(COL_BLOCKS):
            cols = slice(b * CHUNK_COLS, (b + 1) * CHUNK_COLS)
            hi, mid, lo = (terms_ref[i * RANK : (i + 1) * RANK, cols] for i in range(3))
            terms = jnp.concatenate([hi, mid, lo, hi, mid, hi], axis=0)
            recon = jnp.dot(w, terms, preferred_element_type=jnp.float32)
            update_at[n, b] = recon.astype(jnp.bfloat16)
            errors_at[n, b] = (corrected_ref[:, cols].astype(jnp.float32) - recon).astype(
                jnp.bfloat16
            )
            there = pl.ds(b * CHUNK_COLS, CHUNK_COLS)
            pair = (
                pltpu.make_async_copy(
                    update_at.at[n, b], update_ref.at[m, :, there], sems.at[n, b, 0]
                ),
                pltpu.make_async_copy(
                    errors_at.at[n, b], errors_ref.at[0, m, :, there], sems.at[n, b, 1]
                ),
            )
            for copy in pair:
                copy.start()
            copies.extend(pair)
    for m, mine, inverse in rights:
        right_ref[m] = high(inverse, mine, NT)
    for copy in copies:
        copy.wait()


def final_part(core, ts, *rest):
    hbm = pl.BlockSpec(memory_space=pltpu.HBM)
    return pl.pallas_call(
        final_kernel,
        in_specs=[pl.BlockSpec(memory_space=pltpu.SMEM)] + vmem(10),
        out_specs=[hbm, hbm, pl.BlockSpec(memory_space=pltpu.VMEM)],
        out_shape=[
            jax.ShapeDtypeStruct((2, ROWS, D), jnp.bfloat16),
            jax.ShapeDtypeStruct((1, 2, ROWS, D), jnp.bfloat16),
            jax.ShapeDtypeStruct((2, RANK, ROWS), jnp.float32),
        ],
        scratch_shapes=[
            pltpu.VMEM((2, COL_BLOCKS, ROWS, CHUNK_COLS), jnp.bfloat16),
            pltpu.VMEM((2, COL_BLOCKS, ROWS, CHUNK_COLS), jnp.bfloat16),
            pltpu.SemaphoreType.DMA((2, COL_BLOCKS, 2)),
        ],
        compiler_params=pltpu.CompilerParams(vmem_limit_bytes=24 * MIB),
        cost_estimate=cost(2 * 2 * ROWS * 192 * D, 16 * ROWS * D),
        name="final",
    )(core, *ts, *rest)


def on_device(grads, errors, basis_in):
    core = lax.rem(lax.axis_index("tp"), 2).astype(jnp.int32)
    grads, errors, basis = (
        pltpu.with_memory_space_constraint(a, pltpu.HBM)
        for a in (grads, errors, jnp.swapaxes(basis_in, 1, 2))
    )
    corrected_other, left_other = left_part((1 - core)[None], grads, errors, basis)
    with jax.named_scope("left_core_swap"):
        arrived = permute(left_other, CORE_SWAP)
    corrected_own, left_own = left_part(core[None], grads, errors, basis)
    with jax.named_scope("left_sum"):
        parts = exchange(left_own + arrived)
        part = add_up(parts)
        part = part + permute(part, z_pairs(2))
        part = part + permute(part, z_pairs(6))
        left_own = exchange(jnp.broadcast_to(part[None], (CHUNKS,) + part.shape))
        left_other = permute(left_own, CORE_SWAP)
    t_own, terms_own, gram_own = right_part(left_own, corrected_own)
    t, terms_other = right_part(left_other, corrected_other, t_own)
    with jax.named_scope("right_sum"):
        t2, t3, t1 = (permute(t, first_pairs(k)) for k in (2, 3, 1))
        gram_other, t2 = lax.optimization_barrier((gram_part(terms_other), t2))
        t = (t + t1) + (t3 + t2)
        t2, t3, t1 = (permute(t, second_pairs(k)) for k in (2, 3, 1))
    inverse, gram_inverse = inverses(gram_own, gram_other)
    update, new_errors, right = final_part(
        core[None],
        (t, t1, t3, t2),
        inverse,
        gram_inverse,
        terms_own,
        terms_other,
        corrected_own,
        corrected_other,
    )
    return update, new_errors, jnp.swapaxes(right, 1, 2)


def solution(mesh):
    return jax.shard_map(
        on_device,
        mesh=mesh,
        in_specs=(P("dp", None, "tp", None), P("dp", None, "tp", None), P(None, "tp", None)),
        out_specs=(P(None, "tp", None), P("dp", None, "tp", None), P(None, "tp", None)),
        check_vma=False,
    )
```
